128 devices in a mesh: branch: 8 (over x, core), wide: 16 (over y, z).
Axes of the slice: x: 4, y: 4, z: 4, core: 2. Of those that a mesh axis runs over, the one named last changes fastest.
Arguments:
- x_tokens: bfloat16 [1024, 4096], P(('branch', 'wide')), may hold values from -6 to 6
- out_grad: bfloat16 [1024, 4096], P(('branch', 'wide')), may hold values from -6 to 6
- expert_ids: int32 [1024, 2], P(('branch', 'wide')), may hold values from 0 to 7, all different within a row; in each aligned block of 8 rows (0 to 7, 8 to 15, ...) at most 3 rows name the same one
- gate_probs: float32 [1024, 2], P(('branch', 'wide')), may hold values from 0.2 to 1
- w_gate: bfloat16 [8, 6144, 4096], P('branch', 'wide'), may hold values from -0.09375 to 0.09375
- w_up: bfloat16 [8, 6144, 4096], P('branch', 'wide'), may hold values from -0.09375 to 0.09375
- w_down: bfloat16 [8, 6144, 4096], P('branch', 'wide'), may hold values from -0.078125 to 0.078125
- attn_out: bfloat16 [8, 4096, 4096], P('branch', None, 'wide'), may hold values from -6 to 6
Outputs:
- mixed: bfloat16 [1024, 4096], P(('branch', 'wide'))
- token_grad: bfloat16 [1024, 4096], P(('branch', 'wide'))
- merged_attn: bfloat16 [4096, 4096], P('branch', 'wide')
- grad_gate: bfloat16 [16, 8, 16, 24, 4096], P('wide', 'branch')
- grad_up: bfloat16 [16, 8, 16, 24, 4096], P('wide', 'branch')
- grad_down: bfloat16 [16, 8, 16, 24, 4096], P('wide', 'branch')
The draws below stay inside these ranges and needn't reach their ends.
Inputs may be any that keep to these rules, and one draw needn't show every extreme that they name: `expert_ids`: each row names two different experts. In each aligned block of 8 rows (the tokens of one device) no expert is named by more than 3 routes.
All inputs are finite; a program needn't handle non-finite values.
Results may differ from the reference program's by a relative error of at most 0.017.
Values may be sent and summed in bfloat16 or wider, within the bound.
No kernel may reach another device: no remote copies, remote signals or barrier semaphores. Data moves between devices by JAX's collectives and lax.ppermute only.
A program may use at most 128 MiB of HBM per device.

```python
import math
import jax
import jax.numpy as jnp
import numpy as np
from jax import lax

D = 4096
FF = 6144
TOK_DEV = 8
CAP = 3
TOKENS = 1024
PIECE = 24
N_BRANCH = 8
N_WIDE = 16


def with_spikes(result, stream_key, source, target, parts, factor):
    def block_of(dim):
        return (jnp.arange(result.shape[dim]) // (result.shape[dim] // parts)).reshape((-1,) + (1,) * (result.ndim - 1 - dim))

    first = jax.random.permutation(stream_key, parts)[block_of(target)]
    far = (block_of(target) + parts // 2) % parts
    return jnp.where((block_of(source) == first) | (block_of(source) == far), factor * result, result)


def shard_levels(rng, shape, pieces, low, high):
    level, own = 1.0, jax.random.fold_in(rng, 6)
    for position, blocks in pieces:
        draws = jnp.exp(jax.random.uniform(jax.random.fold_in(own, position), (blocks,), jnp.float32, low / len(pieces), high / len(pieces)))
        level = level * jnp.repeat(draws, shape[position] // blocks).reshape([-1 if axis == position else 1 for axis in range(len(shape))])
    return level


def deal_out(stream_key, own, number, rows, count, top, most, slope):
    order = jax.random.permutation(stream_key, count)
    heavy_load, usual = load_shares(count, rows * top, most, slope, True), load_shares(count, rows * top, most, slope, False)
    places = jnp.arange(count)

    def named(lengths, turn):
        used = int((lengths > 0).sum())
        fixed = max(1, used // 4)
        shifted = fixed + (places - fixed + turn * (used - fixed)) % max(1, count - fixed)
        return jnp.zeros((count,), jnp.int32).at[order[jnp.where(places < fixed, places, shifted)]].set(jnp.asarray(lengths, jnp.int32))

    lengths = jnp.where(number % 4 == 0, named(heavy_load, number // 4), named(usual, number - number // 4 - 1))
    mixed = jax.random.permutation(jax.random.fold_in(own, 3), count)
    giver, receiver = mixed[0:count // 2 * 2:2], mixed[1:count // 2 * 2:2]
    margin = jnp.minimum(lengths[giver] - 1, most - lengths[receiver]) // 2
    margin = jnp.where((giver == order[0]) | (receiver == order[0]) | (lengths[receiver] == 0), 0, jnp.maximum(margin, 0))
    shifted = jax.random.randint(jax.random.fold_in(own, 4), (count // 2,), 0, 1 << 20) % (margin + 1)
    lengths = lengths.at[giver].add(-shifted).at[receiver].add(shifted)
    members = jnp.searchsorted(jnp.cumsum(lengths), jnp.arange(rows * top), side="right").astype(jnp.int32)
    listing = members.reshape(top, rows).T
    listing = listing[jax.random.permutation(jax.random.fold_in(own, 1), rows)]
    turn = jax.random.randint(jax.random.fold_in(own, 2), (rows, 1), 0, top)
    return jnp.take_along_axis(listing, (jnp.arange(top)[None, :] + turn) % top, axis=1)


def load_shares(count, total, bound, lean, full):
    loads = [(1 << 20) // math.isqrt(rank ** lean) + 1 for rank in range(1, count + 1)]
    largest = bound if full else min(bound, max(-(-total // count), total * loads[0] // sum(loads)))
    least = 1 if total - largest >= count - 1 else 0
    given, spare = [largest] + [least] * (count - 1), total - largest - least * (count - 1)
    while spare > 0:
        free = [i for i in range(1, count) if given[i] < largest] or [i for i in range(1, count) if given[i] < bound]
        pool, left = sum([loads[i] for i in free]), spare
        for i in free:
            addition = min(bound - given[i], max(1, left * loads[i] // pool), spare)
            given[i] = given[i] + addition
            spare = spare - addition
    return np.array(given)


def noise(own_key, dims, spread, most, split=(), kind=jnp.bfloat16):
    drawn = jax.random.normal(own_key, dims, jnp.float32) * spread
    if len(split) > 0:
        drawn = shard_levels(own_key, dims, split, -0.22, 0.18) * drawn
    return jnp.clip(drawn, min=-most, max=most).astype(kind)


def heavy_noise(own_key, dims, width, most, pieces, heavy, kind=jnp.bfloat16):
    array = width * jax.random.normal(own_key, dims, jnp.float32)
    if pieces:
        array = array * shard_levels(own_key, dims, pieces, -0.22, 0.18)
    return jnp.clip(with_spikes(array, jax.random.fold_in(own_key, 3), *heavy), -most, most).astype(kind)


def setup_inputs(seed: int = 0) -> dict:
    key_list = jax.random.split(jax.random.key(seed), 9)
    x_tokens = noise(key_list[0], (TOKENS, D), 1.0, 6.0, ((0, 128),))
    out_grad = noise(key_list[1], (TOKENS, D), 1.0, 6.0, ((0, 128),))
    expert_ids_keys = jax.random.split(jax.random.fold_in(key_list[2], 1), TOKENS // TOK_DEV)
    expert_ids_turns = jax.random.permutation(jax.random.fold_in(key_list[2], 3), TOKENS // TOK_DEV)
    expert_ids = jax.vmap(lambda own, number: deal_out(jax.random.fold_in(key_list[2], 2), own, number, TOK_DEV, N_BRANCH, 2, CAP, 2))(expert_ids_keys, expert_ids_turns).reshape((TOKENS, 2))
    gate_probs = jnp.clip(0.2 + 0.8 * jax.random.uniform(key_list[3], (TOKENS, 2), jnp.float32) ** shard_levels(key_list[3], (TOKENS, 2), ((0, 128),), -0.2, 0.2), 0.2, 1.0)
    w_gate = noise(key_list[4], (N_BRANCH, FF, D), D ** -0.5, 0.09375, ((0, 8), (1, 16)))
    w_up = noise(key_list[5], (N_BRANCH, FF, D), D ** -0.5, 0.09375, ((0, 8), (1, 16)))
    w_down = noise(key_list[6], (N_BRANCH, FF, D), FF ** -0.5, 0.078125, ((0, 8), (1, 16)))
    attn_out = heavy_noise(key_list[7], (N_BRANCH, D, D), 1.0, 6.0, ((0, 8), (2, 16)), (0, 1, 8, 2.0))
    return dict(x_tokens=x_tokens, out_grad=out_grad, expert_ids=expert_ids, gate_probs=gate_probs, w_gate=w_gate, w_up=w_up, w_down=w_down, attn_out=attn_out)


def expert_pass(tokens_in, grads_in, gate_w, up_w, down_w):
    contract = (((1,), (1,)), ((), ()))
    over_rows = (((0,), (0,)), ((), ()))
    gate_val = lax.dot_general(tokens_in, gate_w, contract, preferred_element_type=jnp.float32)
    up_val = lax.dot_general(tokens_in, up_w, contract, preferred_element_type=jnp.float32)
    sigmoid_gate = jax.nn.sigmoid(gate_val)
    hidden = (gate_val * sigmoid_gate * up_val).astype(jnp.bfloat16)
    partial_out = jnp.dot(hidden, down_w, preferred_element_type=jnp.float32)
    hidden_grad = lax.dot_general(grads_in, down_w, contract, preferred_element_type=jnp.float32)
    gate_grad = (hidden_grad * up_val * sigmoid_gate * (1.0 + gate_val * (1.0 - sigmoid_gate))).astype(jnp.bfloat16)
    up_grad = (hidden_grad * gate_val * sigmoid_gate).astype(jnp.bfloat16)
    partial_in = jnp.dot(gate_grad, gate_w, preferred_element_type=jnp.float32) + jnp.dot(up_grad, up_w, preferred_element_type=jnp.float32)
    grad_gate = lax.dot_general(gate_grad, tokens_in, over_rows, preferred_element_type=jnp.float32).astype(jnp.bfloat16)
    grad_up = lax.dot_general(up_grad, tokens_in, over_rows, preferred_element_type=jnp.float32).astype(jnp.bfloat16)
    grad_down = lax.dot_general(hidden, grads_in, over_rows, preferred_element_type=jnp.float32).astype(jnp.bfloat16)
    return partial_out, partial_in, grad_gate, grad_up, grad_down


def to_expert_layout(grad):
    copies = N_WIDE // N_BRANCH
    shaped = grad.reshape(N_BRANCH, N_WIDE, N_BRANCH, copies, PIECE, D)
    return shaped.transpose(0, 3, 2, 1, 4, 5).reshape(N_WIDE, N_BRANCH, N_WIDE, PIECE, D)


def reference(x_tokens, out_grad, expert_ids, gate_probs, w_gate, w_up, w_down, attn_out):
    merged_attn = jnp.sum(attn_out.astype(jnp.float32) * (1.0 / N_BRANCH), axis=0).astype(jnp.bfloat16)
    device_count = N_BRANCH * N_WIDE
    flat_ids = expert_ids.reshape(device_count, TOK_DEV * 2)
    marked = (flat_ids[:, :, None] == jnp.arange(N_BRANCH, dtype=jnp.int32)[None, None, :]).astype(jnp.int32)
    before = jnp.cumsum(marked, axis=1) - marked
    slot_index = jnp.sum(before * marked, axis=2).reshape(TOKENS, 2)
    owner = (jnp.arange(TOKENS, dtype=jnp.int32) // TOK_DEV)[:, None]
    row_index = (expert_ids * (device_count * CAP) + owner * CAP + slot_index).reshape(-1).astype(jnp.int32)
    slots_all = N_BRANCH * device_count * CAP
    token_buffer = jnp.zeros((slots_all, D), jnp.bfloat16).at[row_index].set(jnp.repeat(x_tokens, 2, axis=0))
    route_grad = (gate_probs[:, :, None] * out_grad.astype(jnp.float32)[:, None, :]).astype(jnp.bfloat16)
    grad_buffer = jnp.zeros((slots_all, D), jnp.bfloat16).at[row_index].set(route_grad.reshape(TOKENS * 2, D))
    stacked = (token_buffer.reshape(N_BRANCH, device_count * CAP, D), grad_buffer.reshape(N_BRANCH, device_count * CAP, D), w_gate, w_up, w_down)
    partial_out, partial_in, grad_gate, grad_up, grad_down = lax.map(lambda operands: expert_pass(*operands), stacked)
    route_out = partial_out.reshape(slots_all, D)[row_index].reshape(TOKENS, 2, D)
    mixed = jnp.sum(gate_probs[:, :, None] * route_out, axis=1).astype(jnp.bfloat16)
    route_in = partial_in.reshape(slots_all, D)[row_index].reshape(TOKENS, 2, D)
    token_grad = jnp.sum(route_in, axis=1).astype(jnp.bfloat16)
    return mixed, token_grad, merged_attn, to_expert_layout(grad_gate), to_expert_layout(grad_up), to_expert_layout(grad_down)
```

```python
import jax
import jax.numpy as jnp
from jax import lax
from jax.experimental import pallas as pl
from jax.experimental.pallas import tpu as pltpu
from jax.sharding import PartitionSpec as P

F32 = jnp.float32
BF16 = jnp.bfloat16
CAP = 3
LAST = (((1,), (1,)), ((), ()))
FIRST = (((0,), (0,)), ((), ()))
PARAMS = pltpu.CompilerParams(vmem_limit_bytes=56 * 1024 * 1024)


def select_kernel(pick_ref, scale_ref, rows_ref, xb_ref, gb_ref, xe_ref, ge_ref):
    features = rows_ref.shape[-1]
    parts = []
    for u in range(rows_ref.shape[1]):
        rows = rows_ref[:, u].reshape(-1, features)
        got = jnp.dot(pick_ref[u], rows, preferred_element_type=F32)
        parts.append(got * scale_ref[u])
    height = parts[0].shape[0] // 4
    for n, ref in enumerate((xb_ref, gb_ref, xe_ref, ge_ref)):
        both = [part[n * height : (n + 1) * height] for part in parts]
        ref[...] = jnp.concatenate(both, axis=0).astype(BF16)


def select_rows(pick, scale, rows):
    groups, picked, depth = pick.shape
    outer, _, per_block, features = rows.shape
    height = picked // 4
    shape = jax.ShapeDtypeStruct((groups * height, features), BF16)
    spec = pl.BlockSpec((2 * height, features), lambda i: (i, 0))
    return pl.pallas_call(
        select_kernel,
        grid=(groups // 2,),
        in_specs=[
            pl.BlockSpec((2, picked, depth), lambda i: (i, 0, 0)),
            pl.BlockSpec((2, picked, 1), lambda i: (i, 0, 0)),
            pl.BlockSpec((outer, 2, per_block, features), lambda i: (0, i, 0, 0)),
        ],
        out_specs=[spec] * 4,
        out_shape=[shape] * 4,
        compiler_params=PARAMS,
        name="select_rows",
    )(pick, scale, rows)


def forward_kernel(x_ref, wg_ref, wu_ref, wd_ref, gate_ref, up_ref, hid_ref, out_ref, acc):
    step = pl.program_id(0)
    gate = lax.dot_general(wg_ref[...], x_ref[...], LAST, preferred_element_type=F32)
    up = lax.dot_general(wu_ref[...], x_ref[...], LAST, preferred_element_type=F32)
    gate_ref[...] = gate
    up_ref[...] = up
    hid = (gate * jax.nn.sigmoid(gate) * up).astype(BF16)
    hid_ref[...] = hid
    part = lax.dot_general(hid, wd_ref[...], FIRST, preferred_element_type=F32)

    @pl.when(step == 0)
    def _():
        acc[...] = part

    @pl.when(step == pl.num_programs(0) - 1)
    def _():
        out_ref[...] = (acc[...] + part).astype(BF16)


def forward(x, wg, wu, wd):
    slots, features = x.shape
    hidden = wg.shape[0]
    tile = hidden // 2
    wspec = pl.BlockSpec((tile, features), lambda i: (i, 0))
    tspec = pl.BlockSpec((tile, slots), lambda i: (i, 0))
    whole = pl.BlockSpec((slots, features), lambda i: (0, 0))
    return pl.pallas_call(
        forward_kernel,
        grid=(2,),
        in_specs=[whole, wspec, wspec, wspec],
        out_specs=[tspec, tspec, tspec, whole],
        out_shape=[
            jax.ShapeDtypeStruct((hidden, slots), F32),
            jax.ShapeDtypeStruct((hidden, slots), F32),
            jax.ShapeDtypeStruct((hidden, slots), BF16),
            jax.ShapeDtypeStruct((slots, features), BF16),
        ],
        scratch_shapes=[pltpu.VMEM((slots, features), F32)],
        compiler_params=PARAMS,
        cost_estimate=pl.CostEstimate(
            flops=6 * slots * features * hidden,
            bytes_accessed=18 * 1024 * 1024,
            transcendentals=slots * hidden,
        ),
        name="expert_forward",
    )(x, wg, wu, wd)


def backward_kernel(
    g_ref, gate_ref, up_ref, hid_ref, wg_ref, wu_ref, wd_ref, send_ref, out_ref, acc
):
    step = pl.program_id(0)
    gate = gate_ref[...]
    up = up_ref[...]
    back = lax.dot_general(wd_ref[...], g_ref[...], LAST, preferred_element_type=F32)
    sig = jax.nn.sigmoid(gate)
    gate_grad = back * up * sig * (1.0 + gate * (1.0 - sig))
    up_grad = back * gate * sig
    pieces, stacked, slots = send_ref.shape
    rows = stacked // 3
    joined = jnp.concatenate(
        [
            gate_grad.reshape(pieces, rows, slots),
            up_grad.reshape(pieces, rows, slots),
            hid_ref[...].astype(F32).reshape(pieces, rows, slots),
        ],
        axis=1,
    )
    send_ref[...] = joined.astype(BF16)
    part = lax.dot_general(
        gate_grad.astype(BF16), wg_ref[...], FIRST, preferred_element_type=F32
    ) + lax.dot_general(up_grad.astype(BF16), wu_ref[...], FIRST, preferred_element_type=F32)

    @pl.when(step == 0)
    def _():
        acc[...] = part

    @pl.when(step == pl.num_programs(0) - 1)
    def _():
        out_ref[...] = (acc[...] + part).astype(BF16)


def backward(g, gate, up, hid, wg, wu, wd, pieces):
    slots, features = g.shape
    hidden = wg.shape[0]
    tile = hidden // 2
    wspec = pl.BlockSpec((tile, features), lambda i: (i, 0))
    tspec = pl.BlockSpec((tile, slots), lambda i: (i, 0))
    whole = pl.BlockSpec((slots, features), lambda i: (0, 0))
    stacked = 3 * hidden // pieces
    return pl.pallas_call(
        backward_kernel,
        grid=(2,),
        in_specs=[whole, tspec, tspec, tspec, wspec, wspec, wspec],
        out_specs=[pl.BlockSpec((pieces // 2, stacked, slots), lambda i: (i, 0, 0)), whole],
        out_shape=[
            jax.ShapeDtypeStruct((pieces, stacked, slots), BF16),
            jax.ShapeDtypeStruct((slots, features), BF16),
        ],
        scratch_shapes=[pltpu.VMEM((slots, features), F32)],
        compiler_params=PARAMS,
        cost_estimate=pl.CostEstimate(
            flops=6 * slots * features * hidden,
            bytes_accessed=18 * 1024 * 1024,
            transcendentals=slots * hidden,
        ),
        name="expert_backward",
    )(g, gate, up, hid, wg, wu, wd)


def weights_kernel(lhs_ref, x_ref, g_ref, gate_ref, up_ref, down_ref):
    pieces, stacked, slots = lhs_ref.shape
    rows = stacked // 3
    lhs = lhs_ref[...].astype(F32)

    def part(n):
        return lhs[:, n * rows : (n + 1) * rows].reshape(pieces * rows, slots).astype(BF16)

    for n, (src, dst) in enumerate(((x_ref, gate_ref), (x_ref, up_ref), (g_ref, down_ref))):
        dst[...] = jnp.dot(part(n), src[...], preferred_element_type=F32).astype(BF16)


def weight_grads(lhs, x, g):
    pieces, stacked, slots = lhs.shape
    features = x.shape[1]
    rows = stacked // 3
    group = 4
    whole = pl.BlockSpec((slots, features), lambda i: (0, 0))
    ospec = pl.BlockSpec((group * rows, features), lambda i: (i, 0))
    oshape = jax.ShapeDtypeStruct((pieces * rows, features), BF16)
    return pl.pallas_call(
        weights_kernel,
        grid=(pieces // group,),
        in_specs=[pl.BlockSpec((group, stacked, slots), lambda i: (i, 0, 0)), whole, whole],
        out_specs=[ospec] * 3,
        out_shape=[oshape] * 3,
        compiler_params=PARAMS,
        cost_estimate=pl.CostEstimate(
            flops=6 * slots * features * pieces * rows,
            bytes_accessed=16 * 1024 * 1024,
            transcendentals=0,
        ),
        name="weight_grads",
    )(lhs, x, g)


def route_pick(ids, probs, expert):
    named = ids == expert
    mine = jnp.any(named, axis=2)
    weight = jnp.sum(jnp.where(named, probs, 0.0), axis=2)
    tokens = ids.shape[1]
    earlier = jnp.arange(tokens)[:, None] < jnp.arange(tokens)[None, :]
    slot = jnp.sum(mine[:, :, None] & earlier[None], axis=1)
    chosen = mine[:, None, :] & (slot[:, None, :] == jnp.arange(CAP)[None, :, None])
    return chosen, jnp.sum(jnp.where(chosen, weight[:, None, :], 0.0), axis=2)


def exchange(value, axis):
    return lax.all_to_all(value, axis, split_axis=0, concat_axis=0, tiled=True)


def on_device(x_tokens, out_grad, expert_ids, gate_probs, w_gate, w_up, w_down, attn_out):
    experts = lax.axis_size("branch")
    wide = lax.axis_size("wide")
    blocks = experts * wide
    tokens, features = x_tokens.shape
    both = ("branch", "wide")
    branch_index = lax.axis_index("branch")
    wide_index = lax.axis_index("wide")

    gathered = lax.all_gather(
        jnp.concatenate([x_tokens, out_grad], axis=0), both, axis=0, tiled=True
    )
    gathered = gathered.reshape(experts, wide, 2 * tokens, features)

    meta = jnp.concatenate([expert_ids.astype(F32), gate_probs], axis=1)
    meta = jnp.pad(meta, ((0, 0), (0, 124)))
    meta = exchange(jnp.broadcast_to(meta[None], (blocks,) + meta.shape), both)
    ids = meta[:, :, 0:2].astype(jnp.int32)
    probs = meta[:, :, 2:4]

    attn = exchange(attn_out[0].reshape(experts, -1, attn_out.shape[2]), "branch")
    merged_attn = (jnp.sum(attn.astype(F32), axis=0) * (1.0 / experts)).astype(BF16)

    same = jnp.eye(experts, dtype=jnp.bool_)
    picks, scales = [], []
    for expert in (branch_index, wide_index // (wide // experts)):
        chosen, weight = route_pick(ids, probs, expert)
        chosen = chosen.reshape(experts, wide, CAP, tokens).transpose(1, 0, 2, 3)
        weight = weight.reshape(experts, wide, CAP).transpose(1, 0, 2).reshape(wide, experts * CAP)
        spread = chosen[:, :, :, None, None, :] & same[None, :, None, :, None, None]
        for kind in range(2):
            which = (jnp.arange(2) == kind)[None, None, None, None, :, None]
            picks.append((spread & which).reshape(wide, experts * CAP, experts * 2 * tokens))
            scales.append(weight if kind else jnp.ones_like(weight))
    pick = jnp.concatenate(picks, axis=1).astype(BF16)
    scale = jnp.concatenate(scales, axis=1)[:, :, None]
    xb, gb, xe, ge = select_rows(pick, scale, gathered)

    gate, up, hid, part_out = forward(xb, w_gate[0], w_up[0], w_down[0])
    send, part_in = backward(gb, gate, up, hid, w_gate[0], w_up[0], w_down[0], wide)

    def reduced(part):
        got = exchange(part.reshape(wide, experts * CAP, features), "wide")
        return jnp.sum(got.astype(F32), axis=0)

    sum_out = reduced(part_out)
    relayed = exchange(exchange(send, "branch"), "wide")
    sum_in = reduced(part_in)
    grad_gate, grad_up, grad_down = weight_grads(relayed, xe, ge)

    back = jnp.concatenate(
        [sum_out.reshape(experts, CAP, features), sum_in.reshape(experts, CAP, features)], axis=1
    )
    back = exchange(back.reshape(experts, 8 * CAP, features // 4), "branch")
    back = back.reshape(experts, 2, CAP, features)

    eids = expert_ids[None]
    own = [route_pick(eids, gate_probs[None], e)[0][0] for e in range(experts)]
    own = jnp.stack(own)
    named = expert_ids[None] == jnp.arange(experts)[:, None, None]
    own_weight = jnp.sum(jnp.where(named, gate_probs[None], 0.0), axis=2)
    chosen = own.astype(F32)
    mixed = jnp.sum(
        (chosen * own_weight[:, None, :])[:, :, :, None] * back[:, 0][:, :, None, :], axis=(0, 1)
    ).astype(BF16)
    token_grad = jnp.sum(chosen[:, :, :, None] * back[:, 1][:, :, None, :], axis=(0, 1)).astype(
        BF16
    )
    layout = (1, 1, wide, w_gate.shape[1] // wide, features)
    return (
        mixed,
        token_grad,
        merged_attn,
        grad_gate.reshape(layout),
        grad_up.reshape(layout),
        grad_down.reshape(layout),
    )


def solution(mesh):
    in_specs = (
        P(("branch", "wide"), None),
        P(("branch", "wide"), None),
        P(("branch", "wide"), None),
        P(("branch", "wide"), None),
        P("branch", "wide", None),
        P("branch", "wide", None),
        P("branch", "wide", None),
        P("branch", None, "wide"),
    )
    out_specs = (
        P(("branch", "wide"), None),
        P(("branch", "wide"), None),
        P("branch", "wide"),
        P("wide", "branch", None, None, None),
        P("wide", "branch", None, None, None),
        P("wide", "branch", None, None, None),
    )
    return jax.shard_map(
        on_device, mesh=mesh, in_specs=in_specs, out_specs=out_specs, check_vma=False
    )
```

```python
import functools

import jax
import jax.numpy as jnp
from jax import lax
from jax.experimental import pallas as pl
from jax.experimental.pallas import tpu as pltpu
from jax.sharding import PartitionSpec as P

F32 = jnp.float32
BF16 = jnp.bfloat16
CAP = 3
LAST = (((1,), (1,)), ((), ()))
PARAMS = pltpu.CompilerParams(vmem_limit_bytes=58 * 1024 * 1024)


def split_rows(rows_ref):
    blocks, per_block, lanes = rows_ref.shape
    half = per_block // 2
    rows = rows_ref[...]
    x = rows[:, :half].reshape(blocks * half, lanes)
    g = rows[:, half:].reshape(blocks * half, lanes)
    return x, g


def one_hot_rows(place, count):
    row = lax.broadcasted_iota(jnp.int32, (count, place.shape[1]), 0)
    return jnp.where(row == place, 1.0, 0.0).astype(BF16)


def expert_kernel(
    place_ref, prob_ref, rows_ref, wg_ref, wu_ref, wd_ref,
    send_ref, back_ref,
    gate_acc, up_acc, hg_acc, acts, results, *, steps, groups,
):
    step = pl.program_id(0)
    slots = acts.shape[1]
    blocks = slots // CAP

    @pl.when(step < steps)
    def _():
        x, g = split_rows(rows_ref)
        for acc, lhs, w_ref in ((gate_acc, x, wg_ref), (up_acc, x, wu_ref), (hg_acc, g, wd_ref)):
            part = lax.dot_general(lhs, w_ref[...], LAST, preferred_element_type=F32)

            @pl.when(step == 0)
            def _(acc=acc, part=part):
                acc[...] = part

            @pl.when(step > 0)
            def _(acc=acc, part=part):
                acc[...] += part

    @pl.when(step == steps)
    def _():
        prob = prob_ref[...]
        gate = gate_acc[...]
        up = up_acc[...]
        sig = jax.nn.sigmoid(gate)
        back = hg_acc[...] * prob
        gate_sig = gate * sig
        pick = one_hot_rows(place_ref[...], slots)
        values = (
            back * up * sig * (1.0 + gate * (1.0 - sig)),
            back * gate_sig,
            gate_sig * up * prob,
        )
        pieces, stacked, _ = send_ref.shape
        height = stacked // 3
        turned = []
        for n, value in enumerate(values):
            got = jnp.dot(pick, value.astype(BF16), preferred_element_type=F32)
            acts[n] = got.astype(BF16)
            turned.append(got.T.reshape(pieces, height, slots))
        send_ref[...] = jnp.concatenate(turned, axis=1).astype(BF16)

    @pl.when((step >= steps) & (step < 2 * steps))
    def _():
        tile = step - steps
        out = jnp.dot(acts[2], wd_ref[...], preferred_element_type=F32)
        results[tile, 0] = out.astype(BF16)
        grad = jnp.dot(acts[0], wg_ref[...], preferred_element_type=F32) + jnp.dot(
            acts[1], wu_ref[...], preferred_element_type=F32
        )
        results[tile, 1] = grad.astype(BF16)

    @pl.when(step >= 2 * steps)
    def _():
        group = step - 2 * steps
        count = blocks // groups
        size = 8 * count
        row = lax.broadcasted_iota(jnp.int32, (size, size), 0)
        column = lax.broadcasted_iota(jnp.int32, (size, size), 1)
        turn = jnp.where(column == (row % 8) * count + row // 8, 1.0, 0.0).astype(BF16)
        pieces = [(o, s, j) for o in range(2) for s in range(CAP) for j in range(steps)]
        done = []
        for n in range(0, len(pieces), 8):
            slab = jnp.concatenate(
                [
                    results[j, o, pl.ds(pl.multiple_of(s * blocks + group * count, count), count), :]
                    for o, s, j in pieces[n : n + 8]
                ],
                axis=0,
            )
            mixed = jnp.dot(turn, slab, preferred_element_type=F32)
            done.append(mixed.reshape(count, 8, mixed.shape[1]))
        back_ref[...] = jnp.concatenate(done, axis=1).astype(BF16)


def expert(place, prob, rows, wg, wu, wd, pieces):
    blocks, per_block, features = rows.shape
    hidden = wg.shape[0]
    slots = blocks * CAP
    tokens = place.shape[1]
    steps, groups = 4, 4
    tile = features // steps

    def wtile(i):
        return (0, jnp.where(i < steps, i, jnp.minimum(i - steps, steps - 1)))

    wspec = pl.BlockSpec((hidden, tile), wtile)
    stacked = 3 * hidden // pieces
    return pl.pallas_call(
        functools.partial(expert_kernel, steps=steps, groups=groups),
        grid=(2 * steps + groups,),
        in_specs=[
            pl.BlockSpec((1, tokens), lambda i: (0, 0)),
            pl.BlockSpec((tokens, 1), lambda i: (0, 0)),
            pl.BlockSpec((blocks, per_block, tile), lambda i: (0, 0, jnp.minimum(i, steps - 1))),
            wspec, wspec, wspec,
        ],
        out_specs=[
            pl.BlockSpec((pieces, stacked, slots), lambda i: (0, 0, 0)),
            pl.BlockSpec(
                (blocks // groups, 8 * CAP, tile), lambda i: (jnp.maximum(i - 2 * steps, 0), 0, 0)
            ),
        ],
        out_shape=[
            jax.ShapeDtypeStruct((pieces, stacked, slots), BF16),
            jax.ShapeDtypeStruct((blocks, 8 * CAP, tile), BF16),
        ],
        scratch_shapes=[
            pltpu.VMEM((tokens, hidden), F32),
            pltpu.VMEM((tokens, hidden), F32),
            pltpu.VMEM((tokens, hidden), F32),
            pltpu.VMEM((3, slots, hidden), BF16),
            pltpu.VMEM((steps, 2, slots, tile), BF16),
        ],
        compiler_params=PARAMS,
        cost_estimate=pl.CostEstimate(
            flops=6 * tokens * features * hidden,
            bytes_accessed=42 * 1024 * 1024,
            transcendentals=tokens * hidden,
        ),
        name="expert",
    )(place, prob, rows, wg, wu, wd)


def pick_kernel(place_ref, rows_ref, x_ref, g_ref):
    x, g = split_rows(rows_ref)
    pick = one_hot_rows(place_ref[...], x_ref.shape[0])
    x_ref[...] = jnp.dot(pick, x, preferred_element_type=F32).astype(BF16)
    g_ref[...] = jnp.dot(pick, g, preferred_element_type=F32).astype(BF16)


def pick_rows(place, rows):
    blocks, per_block, features = rows.shape
    slots = blocks * CAP
    tokens = place.shape[1]
    steps = 4
    tile = features // steps
    spec = pl.BlockSpec((slots, tile), lambda i: (0, i))
    return pl.pallas_call(
        pick_kernel,
        grid=(steps,),
        in_specs=[
            pl.BlockSpec((1, tokens), lambda i: (0, 0)),
            pl.BlockSpec((blocks, per_block, tile), lambda i: (0, 0, i)),
        ],
        out_specs=[spec, spec],
        out_shape=[jax.ShapeDtypeStruct((slots, features), BF16)] * 2,
        compiler_params=PARAMS,
        cost_estimate=pl.CostEstimate(
            flops=4 * slots * tokens * features, bytes_accessed=24 * 1024 * 1024, transcendentals=0
        ),
        name="pick_rows",
    )(place, rows)


def combine_kernel(chosen_ref, got_ref, mixed_ref, grad_ref, acc):
    step = pl.program_id(0)
    total = jnp.sum(got_ref[0].astype(F32), axis=0)
    chosen = chosen_ref[0]
    tile = total.shape[1]
    tiles = mixed_ref.shape[1] // tile

    @pl.when(step == 0)
    def _():
        acc[...] = jnp.zeros_like(acc)

    for o in range(2):
        for j in range(tiles):
            part = acc[o, :, j * tile : (j + 1) * tile]
            for s in range(CAP):
                row = (o * CAP + s) * tiles + j
                part = part + chosen[:, s : s + 1] * total[row : row + 1]
            acc[o, :, j * tile : (j + 1) * tile] = part

    @pl.when(step == pl.num_programs(0) - 1)
    def _():
        mixed_ref[...] = acc[0].astype(BF16)
        grad_ref[...] = acc[1].astype(BF16)


def combine(chosen, got):
    experts, wide, rows, tile = got.shape
    tokens = chosen.shape[1]
    features = tile * rows // (2 * CAP)
    spec = pl.BlockSpec((tokens, features), lambda i: (0, 0))
    return pl.pallas_call(
        combine_kernel,
        grid=(experts,),
        in_specs=[
            pl.BlockSpec((1, tokens, CAP), lambda i: (i, 0, 0)),
            pl.BlockSpec((1, wide, rows, tile), lambda i: (i, 0, 0, 0)),
        ],
        out_specs=[spec, spec],
        out_shape=[jax.ShapeDtypeStruct((tokens, features), BF16)] * 2,
        scratch_shapes=[pltpu.VMEM((2, tokens, features), F32)],
        compiler_params=PARAMS,
        name="combine",
    )(chosen, got)


def weights_kernel(lhs_ref, x_ref, g_ref, gate_ref, up_ref, down_ref):
    pieces, stacked, slots = lhs_ref.shape
    rows = stacked // 3
    lhs = lhs_ref[...].astype(F32)
    for n, (src, dst) in enumerate(((x_ref, gate_ref), (x_ref, up_ref), (g_ref, down_ref))):
        part = lhs[:, n * rows : (n + 1) * rows].reshape(pieces * rows, slots).astype(BF16)
        dst[...] = jnp.dot(part, src[...], preferred_element_type=F32).astype(BF16)


def weight_grads(lhs, x, g):
    pieces, stacked, slots = lhs.shape
    features = x.shape[1]
    rows = stacked // 3
    tile = features // 8
    ispec = pl.BlockSpec((slots, tile), lambda i: (0, i))
    ospec = pl.BlockSpec((pieces * rows, tile), lambda i: (0, i))
    oshape = jax.ShapeDtypeStruct((pieces * rows, features), BF16)
    return pl.pallas_call(
        weights_kernel,
        grid=(features // tile,),
        in_specs=[pl.BlockSpec((pieces, stacked, slots), lambda i: (0, 0, 0)), ispec, ispec],
        out_specs=[ospec] * 3,
        out_shape=[oshape] * 3,
        compiler_params=PARAMS,
        cost_estimate=pl.CostEstimate(
            flops=6 * slots * features * pieces * rows,
            bytes_accessed=16 * 1024 * 1024,
            transcendentals=0,
        ),
        name="weight_grads",
    )(lhs, x, g)


def route_places(ids, probs, expert):
    named = ids == expert
    mine = jnp.any(named, axis=2)
    weight = jnp.sum(jnp.where(named, probs, 0.0), axis=2)
    blocks, tokens = mine.shape
    earlier = jnp.arange(tokens)[:, None] < jnp.arange(tokens)[None, :]
    slot = jnp.sum(mine[:, :, None] & earlier[None], axis=1)
    place = jnp.where(mine, slot * blocks + jnp.arange(blocks)[:, None], -1)
    return place.astype(jnp.int32).reshape(1, blocks * tokens), weight


def exchange(value, axis):
    return lax.all_to_all(value, axis, split_axis=0, concat_axis=0, tiled=True)


def on_device(x_tokens, out_grad, expert_ids, gate_probs, w_gate, w_up, w_down, attn_out):
    experts = lax.axis_size("branch")
    wide = lax.axis_size("wide")
    blocks = experts * wide
    tokens, features = x_tokens.shape
    both = ("branch", "wide")
    branch_index = lax.axis_index("branch")
    wide_index = lax.axis_index("wide")

    gathered = lax.all_gather(
        jnp.concatenate([x_tokens, out_grad], axis=0), both, axis=0, tiled=True
    )
    gathered = gathered.reshape(blocks, 2 * tokens, features)

    meta = jnp.concatenate([expert_ids.astype(F32), gate_probs], axis=1)
    meta = jnp.pad(meta, ((0, 0), (0, 124)))
    meta = exchange(jnp.broadcast_to(meta[None], (blocks,) + meta.shape), both)
    ids = meta[:, :, 0:2].astype(jnp.int32)
    probs = meta[:, :, 2:4]
    place, weight = route_places(ids, probs, branch_index)
    other_place, _ = route_places(ids, probs, wide_index // (wide // experts))

    attn = exchange(attn_out[0].reshape(experts, -1, attn_out.shape[2]), "branch")
    merged_attn = (jnp.sum(attn.astype(F32), axis=0) * (1.0 / experts)).astype(BF16)
    gathered, merged_attn = lax.optimization_barrier((gathered, merged_attn))

    send, back = expert(
        place, weight.reshape(-1, 1), gathered, w_gate[0], w_up[0], w_down[0], wide
    )

    spread = lax.all_gather(send, "branch", axis=0, tiled=True)
    spread = spread.reshape((experts, wide) + send.shape[1:])
    copies = wide // experts
    mine = lax.dynamic_slice_in_dim(spread, branch_index * copies, copies, 1)
    xe, ge = pick_rows(other_place, gathered)
    mine, xe, ge = lax.optimization_barrier((mine.reshape(send.shape), xe, ge))
    relayed = exchange(mine, "wide")

    got = exchange(back, both).reshape(experts, wide, 8 * CAP, -1)

    named = jnp.any(expert_ids[None] == jnp.arange(experts)[:, None, None], axis=2)
    earlier = jnp.arange(tokens)[:, None] < jnp.arange(tokens)[None, :]
    slot = jnp.sum(named[:, :, None] & earlier[None], axis=1)
    chosen = named[:, :, None] & (slot[:, :, None] == jnp.arange(CAP)[None, None, :])
    mixed, token_grad = combine(chosen.astype(F32), got)
    grad_gate, grad_up, grad_down = weight_grads(relayed, xe, ge)

    layout = (1, 1, wide, w_gate.shape[1] // wide, features)
    return (
        mixed,
        token_grad,
        merged_attn,
        grad_gate.reshape(layout),
        grad_up.reshape(layout),
        grad_down.reshape(layout),
    )


def solution(mesh):
    in_specs = (
        P(("branch", "wide"), None),
        P(("branch", "wide"), None),
        P(("branch", "wide"), None),
        P(("branch", "wide"), None),
        P("branch", "wide", None),
        P("branch", "wide", None),
        P("branch", "wide", None),
        P("branch", None, "wide"),
    )
    out_specs = (
        P(("branch", "wide"), None),
        P(("branch", "wide"), None),
        P("branch", "wide"),
        P("wide", "branch", None, None, None),
        P("wide", "branch", None, None, None),
        P("wide", "branch", None, None, None),
    )
    return jax.shard_map(
        on_device, mesh=mesh, in_specs=in_specs, out_specs=out_specs, check_vma=False
    )
```

```python
import functools

import jax
import jax.numpy as jnp
from jax import lax
from jax.experimental import pallas as pl
from jax.experimental.pallas import tpu as pltpu
from jax.sharding import PartitionSpec as P

F32 = jnp.float32
BF16 = jnp.bfloat16
CAP = 3
SIDE = 4
LAST = (((1,), (1,)), ((), ()))
PARAMS = pltpu.CompilerParams(vmem_limit_bytes=58 * 1024 * 1024)


def split_rows(rows_ref):
    blocks, per_block, lanes = rows_ref.shape
    half = per_block // 2
    rows = rows_ref[...]
    x = rows[:, :half].reshape(blocks * half, lanes)
    g = rows[:, half:].reshape(blocks * half, lanes)
    return x, g


def one_hot_rows(place, count):
    row = lax.broadcasted_iota(jnp.int32, (count, place.shape[1]), 0)
    return jnp.where(row == place, 1.0, 0.0).astype(BF16)


def expert_kernel(
    place_ref, prob_ref, rows_ref, wg_ref, wu_ref, wd_ref,
    send_ref, back_ref,
    gate_acc, up_acc, hg_acc, acts, *, steps,
):
    step = pl.program_id(0)
    slots = acts.shape[1]

    @pl.when(step < steps)
    def _():
        x, g = split_rows(rows_ref)
        for acc, lhs, w_ref in ((gate_acc, x, wg_ref), (up_acc, x, wu_ref), (hg_acc, g, wd_ref)):
            part = lax.dot_general(lhs, w_ref[...], LAST, preferred_element_type=F32)

            @pl.when(step == 0)
            def _(acc=acc, part=part):
                acc[...] = part

            @pl.when(step > 0)
            def _(acc=acc, part=part):
                acc[...] += part

    @pl.when(step == steps)
    def _():
        prob = prob_ref[...]
        gate = gate_acc[...]
        up = up_acc[...]
        sig = jax.nn.sigmoid(gate)
        back = hg_acc[...] * prob
        gate_sig = gate * sig
        pick = one_hot_rows(place_ref[...], slots)
        values = (
            back * up * sig * (1.0 + gate * (1.0 - sig)),
            back * gate_sig,
            gate_sig * up * prob,
        )
        pieces, stacked, _ = send_ref.shape
        height = stacked // 3
        turned = []
        for n, value in enumerate(values):
            got = jnp.dot(pick, value.astype(BF16), preferred_element_type=F32)
            acts[n] = got.astype(BF16)
            turned.append(got.T.reshape(pieces, height, slots))
        send_ref[...] = jnp.concatenate(turned, axis=1).astype(BF16)

    @pl.when(step >= steps)
    def _():
        out = jnp.dot(acts[2], wd_ref[...], preferred_element_type=F32)
        grad = jnp.dot(acts[0], wg_ref[...], preferred_element_type=F32) + jnp.dot(
            acts[1], wu_ref[...], preferred_element_type=F32
        )
        wide, _, height, tile = back_ref.shape
        back_ref[:, 0] = out.reshape(wide, height, tile).astype(BF16)
        back_ref[:, 1] = grad.reshape(wide, height, tile).astype(BF16)


def expert(place, prob, rows, wg, wu, wd, pieces):
    blocks, per_block, features = rows.shape
    hidden = wg.shape[0]
    slots = blocks * CAP
    tokens = place.shape[1]
    steps = 4
    tile = features // steps

    def wtile(i):
        return (0, jnp.where(i < steps, i, i - steps))

    wspec = pl.BlockSpec((hidden, tile), wtile)
    stacked = 3 * hidden // pieces
    return pl.pallas_call(
        functools.partial(expert_kernel, steps=steps),
        grid=(2 * steps,),
        in_specs=[
            pl.BlockSpec((1, tokens), lambda i: (0, 0)),
            pl.BlockSpec((tokens, 1), lambda i: (0, 0)),
            pl.BlockSpec((blocks, per_block, tile), lambda i: (0, 0, jnp.minimum(i, steps - 1))),
            wspec, wspec, wspec,
        ],
        out_specs=[
            pl.BlockSpec((pieces, stacked, slots), lambda i: (0, 0, 0)),
            pl.BlockSpec(
                (pieces, 2, slots // pieces, tile), lambda i: (0, 0, 0, jnp.maximum(i - steps, 0))
            ),
        ],
        out_shape=[
            jax.ShapeDtypeStruct((pieces, stacked, slots), BF16),
            jax.ShapeDtypeStruct((pieces, 2, slots // pieces, features), BF16),
        ],
        scratch_shapes=[
            pltpu.VMEM((tokens, hidden), F32),
            pltpu.VMEM((tokens, hidden), F32),
            pltpu.VMEM((tokens, hidden), F32),
            pltpu.VMEM((3, slots, hidden), BF16),
        ],
        compiler_params=PARAMS,
        cost_estimate=pl.CostEstimate(
            flops=6 * tokens * features * hidden,
            bytes_accessed=42 * 1024 * 1024,
            transcendentals=tokens * hidden,
        ),
        name="expert",
    )(place, prob, rows, wg, wu, wd)


def pick_kernel(place_ref, rows_ref, x_ref, g_ref):
    x, g = split_rows(rows_ref)
    pick = one_hot_rows(place_ref[...], x_ref.shape[0])
    x_ref[...] = jnp.dot(pick, x, preferred_element_type=F32).astype(BF16)
    g_ref[...] = jnp.dot(pick, g, preferred_element_type=F32).astype(BF16)


def pick_rows(place, rows):
    blocks, per_block, features = rows.shape
    slots = blocks * CAP
    tokens = place.shape[1]
    steps = 4
    tile = features // steps
    spec = pl.BlockSpec((slots, tile), lambda i: (0, i))
    return pl.pallas_call(
        pick_kernel,
        grid=(steps,),
        in_specs=[
            pl.BlockSpec((1, tokens), lambda i: (0, 0)),
            pl.BlockSpec((blocks, per_block, tile), lambda i: (0, 0, i)),
        ],
        out_specs=[spec, spec],
        out_shape=[jax.ShapeDtypeStruct((slots, features), BF16)] * 2,
        compiler_params=PARAMS,
        cost_estimate=pl.CostEstimate(
            flops=4 * slots * tokens * features, bytes_accessed=24 * 1024 * 1024, transcendentals=0
        ),
        name="pick_rows",
    )(place, rows)


def gather_kernel(got_ref, ret_ref):
    total = jnp.sum(got_ref[...].astype(F32), axis=0)
    experts, padded, tile = ret_ref.shape
    blank = jnp.zeros((padded // 2 - CAP, tile), F32)
    for block in range(experts):
        rows = []
        for o in range(2):
            rows += [total[o, block * CAP : (block + 1) * CAP], blank]
        ret_ref[block] = jnp.concatenate(rows, axis=0).astype(BF16)


def gather_blocks(got, experts):
    parts, _, height, features = got.shape
    steps = 4
    tile = features // steps
    return pl.pallas_call(
        gather_kernel,
        grid=(steps,),
        in_specs=[pl.BlockSpec((parts, 2, height, tile), lambda i: (0, 0, 0, i))],
        out_specs=pl.BlockSpec((experts, 8, tile), lambda i: (0, 0, i)),
        out_shape=jax.ShapeDtypeStruct((experts, 8, features), BF16),
        compiler_params=PARAMS,
        name="gather_blocks",
    )(got)


def combine_kernel(chosen_ref, got_ref, mixed_ref, grad_ref):
    experts = got_ref.shape[0]
    for o, ref in enumerate((mixed_ref, grad_ref)):
        total = jnp.zeros(ref.shape, F32)
        for e in range(experts):
            rows = got_ref[e].astype(F32)
            chosen = chosen_ref[e]
            for s in range(CAP):
                total = total + chosen[:, s : s + 1] * rows[4 * o + s : 4 * o + s + 1]
        ref[...] = total.astype(BF16)


def combine(chosen, got):
    experts, padded, features = got.shape
    tokens = chosen.shape[1]
    steps = 2
    tile = features // steps
    spec = pl.BlockSpec((tokens, tile), lambda i: (0, i))
    return pl.pallas_call(
        combine_kernel,
        grid=(steps,),
        in_specs=[
            pl.BlockSpec((experts, tokens, CAP), lambda i: (0, 0, 0)),
            pl.BlockSpec((experts, padded, tile), lambda i: (0, 0, i)),
        ],
        out_specs=[spec, spec],
        out_shape=[jax.ShapeDtypeStruct((tokens, features), BF16)] * 2,
        compiler_params=PARAMS,
        name="combine",
    )(chosen, got)


def weights_kernel(lhs_ref, x_ref, g_ref, gate_ref, up_ref, down_ref):
    pieces, stacked, slots = lhs_ref.shape
    rows = stacked // 3
    lhs = lhs_ref[...].astype(F32)
    for n, (src, dst) in enumerate(((x_ref, gate_ref), (x_ref, up_ref), (g_ref, down_ref))):
        part = lhs[:, n * rows : (n + 1) * rows].reshape(pieces * rows, slots).astype(BF16)
        dst[...] = jnp.dot(part, src[...], preferred_element_type=F32).astype(BF16)


def weight_grads(lhs, x, g):
    pieces, stacked, slots = lhs.shape
    features = x.shape[1]
    rows = stacked // 3
    tile = features // 8
    ispec = pl.BlockSpec((slots, tile), lambda i: (0, i))
    ospec = pl.BlockSpec((pieces * rows, tile), lambda i: (0, i))
    oshape = jax.ShapeDtypeStruct((pieces * rows, features), BF16)
    return pl.pallas_call(
        weights_kernel,
        grid=(features // tile,),
        in_specs=[pl.BlockSpec((pieces, stacked, slots), lambda i: (0, 0, 0)), ispec, ispec],
        out_specs=[ospec] * 3,
        out_shape=[oshape] * 3,
        compiler_params=PARAMS,
        cost_estimate=pl.CostEstimate(
            flops=6 * slots * features * pieces * rows,
            bytes_accessed=16 * 1024 * 1024,
            transcendentals=0,
        ),
        name="weight_grads",
    )(lhs, x, g)


def route_places(ids, probs, expert, wide):
    named = ids == expert
    mine = jnp.any(named, axis=2)
    weight = jnp.sum(jnp.where(named, probs, 0.0), axis=2)
    blocks, tokens = mine.shape
    earlier = jnp.arange(tokens)[:, None] < jnp.arange(tokens)[None, :]
    slot = jnp.sum(mine[:, :, None] & earlier[None], axis=1)
    block = jnp.arange(blocks)
    column, branch = block % wide, block // wide
    turned = column % SIDE * SIDE + column // SIDE
    group = jnp.where(expert % 2 == 0, column, turned)
    start = (group * (blocks // wide) + branch) * CAP
    place = jnp.where(mine, start[:, None] + slot, -1)
    return place.astype(jnp.int32).reshape(1, blocks * tokens), weight


def stage_groups(experts, wide, odd):
    groups = []
    for branch in range(experts):
        for k in range(SIDE):
            fast = branch % 2 != odd
            members = [k * SIDE + n if fast else n * SIDE + k for n in range(SIDE)]
            groups.append([branch * wide + m for m in members])
    return groups


def exchange(value, axis):
    return lax.all_to_all(value, axis, split_axis=0, concat_axis=0, tiled=True)


def on_device(x_tokens, out_grad, expert_ids, gate_probs, w_gate, w_up, w_down, attn_out):
    experts = lax.axis_size("branch")
    wide = lax.axis_size("wide")
    blocks = experts * wide
    tokens, features = x_tokens.shape
    both = ("branch", "wide")
    branch_index = lax.axis_index("branch")
    wide_index = lax.axis_index("wide")

    gathered = lax.all_gather(
        jnp.concatenate([x_tokens, out_grad], axis=0), both, axis=0, tiled=True
    )
    gathered = gathered.reshape(blocks, 2 * tokens, features)

    meta = jnp.concatenate([expert_ids.astype(F32), gate_probs], axis=1)
    meta = jnp.pad(meta, ((0, 0), (0, 124)))
    meta = exchange(jnp.broadcast_to(meta[None], (blocks,) + meta.shape), both)
    ids = meta[:, :, 0:2].astype(jnp.int32)
    probs = meta[:, :, 2:4]
    place, weight = route_places(ids, probs, branch_index, wide)
    other_place, _ = route_places(ids, probs, wide_index // (wide // experts), wide)

    attn = exchange(attn_out[0].reshape(experts, -1, attn_out.shape[2]), "branch")
    merged_attn = (jnp.sum(attn.astype(F32), axis=0) * (1.0 / experts)).astype(BF16)
    gathered, merged_attn = lax.optimization_barrier((gathered, merged_attn))

    send, back = expert(
        place, weight.reshape(-1, 1), gathered, w_gate[0], w_up[0], w_down[0], wide
    )

    spread = lax.all_gather(send, "branch", axis=0, tiled=True)
    spread = spread.reshape((experts, wide) + send.shape[1:])
    copies = wide // experts
    mine = lax.dynamic_slice_in_dim(spread, branch_index * copies, copies, 1)
    def stage(value, odd):
        return lax.all_to_all(
            value,
            both,
            split_axis=0,
            concat_axis=0,
            axis_index_groups=stage_groups(experts, wide, odd),
            tiled=True,
        )

    first = stage(back, 0)
    xe, ge = pick_rows(other_place, gathered)
    first, mine, xe, ge = lax.optimization_barrier((first, mine.reshape(send.shape), xe, ge))
    relayed = exchange(mine, "wide")
    first = first.reshape((SIDE, SIDE) + back.shape[1:])
    second = jnp.sum(first.astype(F32), axis=0).astype(BF16)
    second, relayed = lax.optimization_barrier((second, relayed))
    returned = gather_blocks(stage(second, 1), experts)
    grad_gate, grad_up, grad_down = weight_grads(relayed, xe, ge)
    got = exchange(returned, "branch")

    named = jnp.any(expert_ids[None] == jnp.arange(experts)[:, None, None], axis=2)
    earlier = jnp.arange(tokens)[:, None] < jnp.arange(tokens)[None, :]
    slot = jnp.sum(named[:, :, None] & earlier[None], axis=1)
    chosen = named[:, :, None] & (slot[:, :, None] == jnp.arange(CAP)[None, None, :])
    mixed, token_grad = combine(chosen.astype(F32), got)

    layout = (1, 1, wide, w_gate.shape[1] // wide, features)
    return (
        mixed,
        token_grad,
        merged_attn,
        grad_gate.reshape(layout),
        grad_up.reshape(layout),
        grad_down.reshape(layout),
    )


def solution(mesh):
    in_specs = (
        P(("branch", "wide"), None),
        P(("branch", "wide"), None),
        P(("branch", "wide"), None),
        P(("branch", "wide"), None),
        P("branch", "wide", None),
        P("branch", "wide", None),
        P("branch", "wide", None),
        P("branch", None, "wide"),
    )
    out_specs = (
        P(("branch", "wide"), None),
        P(("branch", "wide"), None),
        P("branch", "wide"),
        P("wide", "branch", None, None, None),
        P("wide", "branch", None, None, None),
        P("wide", "branch", None, None, None),
    )
    return jax.shard_map(
        on_device, mesh=mesh, in_specs=in_specs, out_specs=out_specs, check_vma=False
    )
```

```python
import functools

import jax
import jax.numpy as jnp
from jax import lax
from jax.experimental import pallas as pl
from jax.experimental.pallas import tpu as pltpu
from jax.sharding import PartitionSpec as P

F32 = jnp.float32
BF16 = jnp.bfloat16
CAP = 3
SIDE = 4
LAST = (((1,), (1,)), ((), ()))
PARAMS = pltpu.CompilerParams(vmem_limit_bytes=58 * 1024 * 1024)


SMALL = pltpu.CompilerParams(vmem_limit_bytes=16 * 1024 * 1024)


def split_rows(rows_ref):
    blocks, per_block, lanes = rows_ref.shape
    half = per_block // 2
    rows = rows_ref[...]
    x = rows[:, :half].reshape(blocks * half, lanes)
    g = rows[:, half:].reshape(blocks * half, lanes)
    return x, g


def one_hot_rows(place, count):
    row = lax.broadcasted_iota(jnp.int32, (count, place.shape[1]), 0)
    return jnp.where(row == place, 1.0, 0.0).astype(BF16)


def expert_kernel(
    place_ref, prob_ref, rows_ref, wg_ref, wu_ref, wd_ref,
    send_ref, back_ref,
    gate_acc, up_acc, hg_acc, acts, kept, *, steps,
):
    step = pl.program_id(0)
    slots = acts.shape[1]

    @pl.when(step < steps)
    def _():
        x, g = split_rows(rows_ref)
        ops = ((gate_acc, x, wg_ref), (up_acc, x, wu_ref), (hg_acc, g, wd_ref))
        for n, (acc, rhs, w_ref) in enumerate(ops):
            w = w_ref[...]
            kept[step, n] = w
            part = lax.dot_general(w, rhs, LAST, preferred_element_type=F32)

            @pl.when(step == 0)
            def _(acc=acc, part=part):
                acc[...] = part

            @pl.when(step > 0)
            def _(acc=acc, part=part):
                acc[...] += part

    @pl.when(step == steps)
    def _():
        prob = prob_ref[...]
        gate = gate_acc[...]
        up = up_acc[...]
        sig = jax.nn.sigmoid(gate)
        back = hg_acc[...] * prob
        gate_sig = gate * sig
        pick = one_hot_rows(place_ref[...], slots)
        values = (
            back * up * sig * (1.0 + gate * (1.0 - sig)),
            back * gate_sig,
            gate_sig * up * prob,
        )
        pieces, stacked, _ = send_ref.shape
        height = stacked // 3
        turned = []
        for n, value in enumerate(values):
            got = lax.dot_general(value.astype(BF16), pick, LAST, preferred_element_type=F32)
            acts[n] = got.T.astype(BF16)
            turned.append(got.reshape(pieces, height, slots))
        send_ref[...] = jnp.concatenate(turned, axis=1).astype(BF16)

    @pl.when(step >= steps)
    def _():
        tile = step - steps
        out = jnp.dot(acts[2], kept[tile, 2], preferred_element_type=F32)
        grad = jnp.dot(acts[0], kept[tile, 0], preferred_element_type=F32) + jnp.dot(
            acts[1], kept[tile, 1], preferred_element_type=F32
        )
        wide, _, height, width = back_ref.shape
        back_ref[:, 0] = out.reshape(wide, height, width).astype(BF16)
        back_ref[:, 1] = grad.reshape(wide, height, width).astype(BF16)


def expert(place, prob, rows, wg, wu, wd, pieces):
    blocks, per_block, features = rows.shape
    hidden = wg.shape[0]
    slots = blocks * CAP
    tokens = place.shape[1]
    steps = 4
    tile = features // steps
    wspec = pl.BlockSpec((hidden, tile), lambda i: (0, jnp.minimum(i, steps - 1)))
    line = pl.BlockSpec((1, tokens), lambda i: (0, 0))
    stacked = 3 * hidden // pieces
    return pl.pallas_call(
        functools.partial(expert_kernel, steps=steps),
        grid=(2 * steps,),
        in_specs=[
            line, line,
            pl.BlockSpec((blocks, per_block, tile), lambda i: (0, 0, jnp.minimum(i, steps - 1))),
            wspec, wspec, wspec,
        ],
        out_specs=[
            pl.BlockSpec((pieces, stacked, slots), lambda i: (0, 0, 0)),
            pl.BlockSpec(
                (pieces, 2, slots // pieces, tile), lambda i: (0, 0, 0, jnp.maximum(i - steps, 0))
            ),
        ],
        out_shape=[
            jax.ShapeDtypeStruct((pieces, stacked, slots), BF16),
            jax.ShapeDtypeStruct((pieces, 2, slots // pieces, features), BF16),
        ],
        scratch_shapes=[
            pltpu.VMEM((hidden, tokens), F32),
            pltpu.VMEM((hidden, tokens), F32),
            pltpu.VMEM((hidden, tokens), F32),
            pltpu.VMEM((3, slots, hidden), BF16),
            pltpu.VMEM((steps, 3, hidden, tile), BF16),
        ],
        compiler_params=PARAMS,
        cost_estimate=pl.CostEstimate(
            flops=6 * tokens * features * hidden,
            bytes_accessed=33 * 1024 * 1024,
            transcendentals=tokens * hidden,
        ),
        name="expert",
    )(place, prob, rows, wg, wu, wd)


def pick_kernel(place_ref, rows_ref, x_ref, g_ref):
    x, g = split_rows(rows_ref)
    pick = one_hot_rows(place_ref[...], x_ref.shape[0])
    x_ref[...] = jnp.dot(pick, x, preferred_element_type=F32).astype(BF16)
    g_ref[...] = jnp.dot(pick, g, preferred_element_type=F32).astype(BF16)


def pick_rows(place, rows):
    blocks, per_block, features = rows.shape
    slots = blocks * CAP
    tokens = place.shape[1]
    steps = 4
    tile = features // steps
    spec = pl.BlockSpec((slots, tile), lambda i: (0, i))
    return pl.pallas_call(
        pick_kernel,
        grid=(steps,),
        in_specs=[
            pl.BlockSpec((1, tokens), lambda i: (0, 0)),
            pl.BlockSpec((blocks, per_block, tile), lambda i: (0, 0, i)),
        ],
        out_specs=[spec, spec],
        out_shape=[jax.ShapeDtypeStruct((slots, features), BF16)] * 2,
        compiler_params=PARAMS,
        cost_estimate=pl.CostEstimate(
            flops=4 * slots * tokens * features, bytes_accessed=24 * 1024 * 1024, transcendentals=0
        ),
        name="pick_rows",
    )(place, rows)


def gather_kernel(got_ref, ret_ref):
    total = jnp.sum(got_ref[...].astype(F32), axis=0)
    experts, padded, tile = ret_ref.shape
    blank = jnp.zeros((padded // 2 - CAP, tile), F32)
    for block in range(experts):
        rows = []
        for o in range(2):
            rows += [total[o, block * CAP : (block + 1) * CAP], blank]
        ret_ref[block] = jnp.concatenate(rows, axis=0).astype(BF16)


def gather_blocks(got, experts):
    parts, _, height, features = got.shape
    steps = 4
    tile = features // steps
    return pl.pallas_call(
        gather_kernel,
        grid=(steps,),
        in_specs=[pl.BlockSpec((parts, 2, height, tile), lambda i: (0, 0, 0, i))],
        out_specs=pl.BlockSpec((experts, 8, tile), lambda i: (0, 0, i)),
        out_shape=jax.ShapeDtypeStruct((experts, 8, features), BF16),
        compiler_params=SMALL,
        name="gather_blocks",
    )(got)


def combine_kernel(chosen_ref, got_ref, mixed_ref, grad_ref):
    experts = got_ref.shape[0]
    for o, ref in enumerate((mixed_ref, grad_ref)):
        total = jnp.zeros(ref.shape, F32)
        for e in range(experts):
            rows = got_ref[e].astype(F32)
            chosen = chosen_ref[e]
            for s in range(CAP):
                total = total + chosen[:, s : s + 1] * rows[4 * o + s : 4 * o + s + 1]
        ref[...] = total.astype(BF16)


def combine(chosen, got):
    experts, padded, features = got.shape
    tokens = chosen.shape[1]
    steps = 2
    tile = features // steps
    spec = pl.BlockSpec((tokens, tile), lambda i: (0, i))
    return pl.pallas_call(
        combine_kernel,
        grid=(steps,),
        in_specs=[
            pl.BlockSpec((experts, tokens, CAP), lambda i: (0, 0, 0)),
            pl.BlockSpec((experts, padded, tile), lambda i: (0, 0, i)),
        ],
        out_specs=[spec, spec],
        out_shape=[jax.ShapeDtypeStruct((tokens, features), BF16)] * 2,
        compiler_params=SMALL,
        name="combine",
    )(chosen, got)


def weights_kernel(lhs_ref, x_ref, g_ref, gate_ref, up_ref, down_ref):
    pieces, stacked, slots = lhs_ref.shape
    rows = stacked // 3
    lhs = lhs_ref[...].astype(F32)
    for n, (src, dst) in enumerate(((x_ref, gate_ref), (x_ref, up_ref), (g_ref, down_ref))):
        part = lhs[:, n * rows : (n + 1) * rows].reshape(pieces * rows, slots).astype(BF16)
        dst[...] = jnp.dot(part, src[...], preferred_element_type=F32).astype(BF16)


def weight_grads(lhs, x, g):
    pieces, stacked, slots = lhs.shape
    features = x.shape[1]
    rows = stacked // 3
    tile = features // 8
    ispec = pl.BlockSpec((slots, tile), lambda i: (0, i))
    ospec = pl.BlockSpec((pieces * rows, tile), lambda i: (0, i))
    oshape = jax.ShapeDtypeStruct((pieces * rows, features), BF16)
    return pl.pallas_call(
        weights_kernel,
        grid=(features // tile,),
        in_specs=[pl.BlockSpec((pieces, stacked, slots), lambda i: (0, 0, 0)), ispec, ispec],
        out_specs=[ospec] * 3,
        out_shape=[oshape] * 3,
        compiler_params=PARAMS,
        cost_estimate=pl.CostEstimate(
            flops=6 * slots * features * pieces * rows,
            bytes_accessed=16 * 1024 * 1024,
            transcendentals=0,
        ),
        name="weight_grads",
    )(lhs, x, g)


def route_places(ids, probs, expert, wide):
    named = ids == expert
    mine = jnp.any(named, axis=2)
    weight = jnp.sum(jnp.where(named, probs, 0.0), axis=2)
    blocks, tokens = mine.shape
    earlier = jnp.arange(tokens)[:, None] < jnp.arange(tokens)[None, :]
    slot = jnp.sum(mine[:, :, None] & earlier[None], axis=1)
    block = jnp.arange(blocks)
    column, branch = block % wide, block // wide
    turned = column % SIDE * SIDE + column // SIDE
    group = jnp.where(expert % 2 == 0, column, turned)
    start = (group * (blocks // wide) + branch) * CAP
    place = jnp.where(mine, start[:, None] + slot, -1)
    return place.astype(jnp.int32).reshape(1, blocks * tokens), weight


def stage_groups(experts, wide, odd):
    groups = []
    for branch in range(experts):
        for k in range(SIDE):
            fast = branch % 2 != odd
            members = [k * SIDE + n if fast else n * SIDE + k for n in range(SIDE)]
            groups.append([branch * wide + m for m in members])
    return groups


def exchange(value, axis):
    return lax.all_to_all(value, axis, split_axis=0, concat_axis=0, tiled=True)


def on_device(x_tokens, out_grad, expert_ids, gate_probs, w_gate, w_up, w_down, attn_out):
    experts = lax.axis_size("branch")
    wide = lax.axis_size("wide")
    blocks = experts * wide
    tokens, features = x_tokens.shape
    both = ("branch", "wide")
    branch_index = lax.axis_index("branch")
    wide_index = lax.axis_index("wide")

    gathered = lax.all_gather(
        jnp.concatenate([x_tokens, out_grad], axis=0), both, axis=0, tiled=True
    )
    gathered = gathered.reshape(blocks, 2 * tokens, features)

    meta = jnp.concatenate([expert_ids.astype(F32), gate_probs], axis=1)
    meta = jnp.pad(meta, ((0, 0), (0, 124)))
    meta = exchange(jnp.broadcast_to(meta[None], (blocks,) + meta.shape), both)
    ids = meta[:, :, 0:2].astype(jnp.int32)
    probs = meta[:, :, 2:4]
    place, weight = route_places(ids, probs, branch_index, wide)
    other_place, _ = route_places(ids, probs, wide_index // (wide // experts), wide)

    scaled = (attn_out[0].astype(F32) * (1.0 / experts)).astype(BF16)
    gathered, scaled = lax.optimization_barrier((gathered, scaled))

    send, back = expert(
        place, weight.reshape(1, -1), gathered, w_gate[0], w_up[0], w_down[0], wide
    )

    spread = lax.all_gather(send, "branch", axis=0, tiled=True)
    xe, ge = pick_rows(other_place, gathered)
    spread, scaled, xe, ge = lax.optimization_barrier((spread, scaled, xe, ge))
    spread = spread.reshape((experts, wide) + send.shape[1:])
    copies = wide // experts
    mine = lax.dynamic_slice_in_dim(spread, branch_index * copies, copies, 1)
    merged_attn = lax.psum_scatter(scaled, "branch", scatter_dimension=0, tiled=True)

    def stage(value, odd):
        return lax.all_to_all(
            value,
            both,
            split_axis=0,
            concat_axis=0,
            axis_index_groups=stage_groups(experts, wide, odd),
            tiled=True,
        )

    first = stage(back, 0)
    first, mine = lax.optimization_barrier((first, mine.reshape(send.shape)))
    relayed = exchange(mine, "wide")
    first = first.reshape((SIDE, SIDE) + back.shape[1:])
    second = jnp.sum(first.astype(F32), axis=0).astype(BF16)
    second, relayed = lax.optimization_barrier((second, relayed))
    returned = gather_blocks(stage(second, 1), experts)
    grad_gate, grad_up, grad_down = weight_grads(relayed, xe, ge)
    got = exchange(returned, "branch")

    named = jnp.any(expert_ids[None] == jnp.arange(experts)[:, None, None], axis=2)
    earlier = jnp.arange(tokens)[:, None] < jnp.arange(tokens)[None, :]
    slot = jnp.sum(named[:, :, None] & earlier[None], axis=1)
    chosen = named[:, :, None] & (slot[:, :, None] == jnp.arange(CAP)[None, None, :])
    mixed, token_grad = combine(chosen.astype(F32), got)

    layout = (1, 1, wide, w_gate.shape[1] // wide, features)
    return (
        mixed,
        token_grad,
        merged_attn,
        grad_gate.reshape(layout),
        grad_up.reshape(layout),
        grad_down.reshape(layout),
    )


def solution(mesh):
    in_specs = (
        P(("branch", "wide"), None),
        P(("branch", "wide"), None),
        P(("branch", "wide"), None),
        P(("branch", "wide"), None),
        P("branch", "wide", None),
        P("branch", "wide", None),
        P("branch", "wide", None),
        P("branch", None, "wide"),
    )
    out_specs = (
        P(("branch", "wide"), None),
        P(("branch", "wide"), None),
        P("branch", "wide"),
        P("wide", "branch", None, None, None),
        P("wide", "branch", None, None, None),
        P("wide", "branch", None, None, None),
    )
    return jax.shard_map(
        on_device, mesh=mesh, in_specs=in_specs, out_specs=out_specs, check_vma=False
    )
```

```python
import functools

import jax
import jax.numpy as jnp
from jax import lax
from jax.experimental import pallas as pl
from jax.experimental.pallas import tpu as pltpu
from jax.sharding import PartitionSpec as P

F32 = jnp.float32
BF16 = jnp.bfloat16
CAP = 3
SIDE = 4
LAST = (((1,), (1,)), ((), ()))
PARAMS = pltpu.CompilerParams(vmem_limit_bytes=58 * 1024 * 1024)


SMALL = pltpu.CompilerParams(vmem_limit_bytes=16 * 1024 * 1024)


def split_rows(rows_ref):
    blocks, per_block, lanes = rows_ref.shape
    half = per_block // 2
    rows = rows_ref[...]
    x = rows[:, :half].reshape(blocks * half, lanes)
    g = rows[:, half:].reshape(blocks * half, lanes)
    return x, g


def one_hot_rows(place, count):
    row = lax.broadcasted_iota(jnp.int32, (count, place.shape[1]), 0)
    return jnp.where(row == place, 1.0, 0.0).astype(BF16)


def expert_kernel(
    place_ref, prob_ref, rows_ref, wg_ref, wu_ref, wd_ref,
    send_ref, back_ref,
    pair_acc, hg_acc, acts, kept, *, steps,
):
    step = pl.program_id(0)
    slots = acts.shape[1]

    @pl.when(step < steps)
    def _():
        x, g = split_rows(rows_ref)
        for n, w_ref in enumerate((wg_ref, wu_ref, wd_ref)):
            kept[step, n] = w_ref[...]
        pair = jnp.concatenate([wg_ref[...], wu_ref[...]], axis=0)
        for acc, w, rhs in ((pair_acc, pair, x), (hg_acc, wd_ref[...], g)):
            part = lax.dot_general(w, rhs, LAST, preferred_element_type=F32)

            @pl.when(step == 0)
            def _(acc=acc, part=part):
                acc[...] = part

            @pl.when(step > 0)
            def _(acc=acc, part=part):
                acc[...] += part

    @pl.when(step == steps)
    def _():
        prob = prob_ref[...]
        hidden = hg_acc.shape[0]
        gate = pair_acc[:hidden]
        up = pair_acc[hidden:]
        sig = jax.nn.sigmoid(gate)
        back = hg_acc[...] * prob
        gate_sig = gate * sig
        pick = one_hot_rows(place_ref[...], slots)
        values = (
            back * up * sig * (1.0 + gate * (1.0 - sig)),
            back * gate_sig,
            gate_sig * up * prob,
        )
        pieces, stacked, _ = send_ref.shape
        height = stacked // 3
        turned = []
        for n, value in enumerate(values):
            got = lax.dot_general(value.astype(BF16), pick, LAST, preferred_element_type=F32)
            acts[n] = got.T.astype(BF16)
            turned.append(got.reshape(pieces, height, slots))
        send_ref[...] = jnp.concatenate(turned, axis=1).astype(BF16)

    @pl.when(step >= steps)
    def _():
        tile = step - steps
        out = jnp.dot(acts[2], kept[tile, 2], preferred_element_type=F32)
        grad = jnp.dot(acts[0], kept[tile, 0], preferred_element_type=F32) + jnp.dot(
            acts[1], kept[tile, 1], preferred_element_type=F32
        )
        wide, _, height, width = back_ref.shape
        back_ref[:, 0] = out.reshape(wide, height, width).astype(BF16)
        back_ref[:, 1] = grad.reshape(wide, height, width).astype(BF16)


def expert(place, prob, rows, wg, wu, wd, pieces):
    blocks, per_block, features = rows.shape
    hidden = wg.shape[0]
    slots = blocks * CAP
    tokens = place.shape[1]
    steps = 4
    tile = features // steps
    wspec = pl.BlockSpec((hidden, tile), lambda i: (0, jnp.minimum(i, steps - 1)))
    line = pl.BlockSpec((1, tokens), lambda i: (0, 0))
    stacked = 3 * hidden // pieces
    return pl.pallas_call(
        functools.partial(expert_kernel, steps=steps),
        grid=(2 * steps,),
        in_specs=[
            line, line,
            pl.BlockSpec((blocks, per_block, tile), lambda i: (0, 0, jnp.minimum(i, steps - 1))),
            wspec, wspec, wspec,
        ],
        out_specs=[
            pl.BlockSpec((pieces, stacked, slots), lambda i: (0, 0, 0)),
            pl.BlockSpec(
                (pieces, 2, slots // pieces, tile), lambda i: (0, 0, 0, jnp.maximum(i - steps, 0))
            ),
        ],
        out_shape=[
            jax.ShapeDtypeStruct((pieces, stacked, slots), BF16),
            jax.ShapeDtypeStruct((pieces, 2, slots // pieces, features), BF16),
        ],
        scratch_shapes=[
            pltpu.VMEM((2 * hidden, tokens), F32),
            pltpu.VMEM((hidden, tokens), F32),
            pltpu.VMEM((3, slots, hidden), BF16),
            pltpu.VMEM((steps, 3, hidden, tile), BF16),
        ],
        compiler_params=PARAMS,
        cost_estimate=pl.CostEstimate(
            flops=6 * tokens * features * hidden,
            bytes_accessed=33 * 1024 * 1024,
            transcendentals=tokens * hidden,
        ),
        name="expert",
    )(place, prob, rows, wg, wu, wd)


def pick_kernel(place_ref, rows_ref, x_ref, g_ref):
    x, g = split_rows(rows_ref)
    pick = one_hot_rows(place_ref[...], x_ref.shape[0])
    x_ref[...] = jnp.dot(pick, x, preferred_element_type=F32).astype(BF16)
    g_ref[...] = jnp.dot(pick, g, preferred_element_type=F32).astype(BF16)


def pick_rows(place, rows):
    blocks, per_block, features = rows.shape
    slots = blocks * CAP
    tokens = place.shape[1]
    steps = 4
    tile = features // steps
    spec = pl.BlockSpec((slots, tile), lambda i: (0, i))
    return pl.pallas_call(
        pick_kernel,
        grid=(steps,),
        in_specs=[
            pl.BlockSpec((1, tokens), lambda i: (0, 0)),
            pl.BlockSpec((blocks, per_block, tile), lambda i: (0, 0, i)),
        ],
        out_specs=[spec, spec],
        out_shape=[jax.ShapeDtypeStruct((slots, features), BF16)] * 2,
        compiler_params=PARAMS,
        cost_estimate=pl.CostEstimate(
            flops=4 * slots * tokens * features, bytes_accessed=24 * 1024 * 1024, transcendentals=0
        ),
        name="pick_rows",
    )(place, rows)


def first_sum_kernel(position_ref, got_ref, *refs):
    total, outs = refs[-1], refs[:-1]
    total[...] = jnp.sum(got_ref[...].astype(F32), axis=0)
    for distance, ref in enumerate(outs):
        ref[...] = total[lax.rem(position_ref[0] + distance, len(outs))].astype(BF16)


def first_sum(position, got):
    parts, _, _, height, features = got.shape
    steps = 4
    tile = features // steps
    return pl.pallas_call(
        first_sum_kernel,
        grid=(steps,),
        in_specs=[
            pl.BlockSpec(memory_space=pltpu.SMEM),
            pl.BlockSpec((parts, parts, 2, height, tile), lambda i: (0, 0, 0, 0, i)),
        ],
        out_specs=[pl.BlockSpec((2, height, tile), lambda i: (0, 0, i))] * parts,
        out_shape=[jax.ShapeDtypeStruct((2, height, features), BF16)] * parts,
        scratch_shapes=[pltpu.VMEM((parts, 2, height, tile), F32)],
        compiler_params=SMALL,
        name="first_sum",
    )(position, got)


def gather_kernel(*refs):
    ret_ref = refs[-1]
    total = sum(ref[...].astype(F32) for ref in refs[:-1])
    experts, padded, tile = ret_ref.shape
    blank = jnp.zeros((padded // 2 - CAP, tile), F32)
    for block in range(experts):
        rows = []
        for o in range(2):
            rows += [total[o, block * CAP : (block + 1) * CAP], blank]
        ret_ref[block] = jnp.concatenate(rows, axis=0).astype(BF16)


def gather_blocks(got, experts):
    _, height, features = got[0].shape
    steps = 4
    tile = features // steps
    return pl.pallas_call(
        gather_kernel,
        grid=(steps,),
        in_specs=[pl.BlockSpec((2, height, tile), lambda i: (0, 0, i))] * len(got),
        out_specs=pl.BlockSpec((experts, 8, tile), lambda i: (0, 0, i)),
        out_shape=jax.ShapeDtypeStruct((experts, 8, features), BF16),
        compiler_params=SMALL,
        name="gather_blocks",
    )(*got)


def combine_kernel(chosen_ref, got_ref, mixed_ref, grad_ref):
    experts = got_ref.shape[0]
    for o, ref in enumerate((mixed_ref, grad_ref)):
        total = jnp.zeros(ref.shape, F32)
        for e in range(experts):
            rows = got_ref[e].astype(F32)
            chosen = chosen_ref[e]
            for s in range(CAP):
                total = total + chosen[:, s : s + 1] * rows[4 * o + s : 4 * o + s + 1]
        ref[...] = total.astype(BF16)


def combine(chosen, got):
    experts, padded, features = got.shape
    tokens = chosen.shape[1]
    steps = 2
    tile = features // steps
    spec = pl.BlockSpec((tokens, tile), lambda i: (0, i))
    return pl.pallas_call(
        combine_kernel,
        grid=(steps,),
        in_specs=[
            pl.BlockSpec((experts, tokens, CAP), lambda i: (0, 0, 0)),
            pl.BlockSpec((experts, padded, tile), lambda i: (0, 0, i)),
        ],
        out_specs=[spec, spec],
        out_shape=[jax.ShapeDtypeStruct((tokens, features), BF16)] * 2,
        compiler_params=SMALL,
        name="combine",
    )(chosen, got)


def weights_kernel(lhs_ref, x_ref, g_ref, gate_ref, up_ref, down_ref):
    pieces, stacked, slots = lhs_ref.shape
    rows = stacked // 3
    lhs = lhs_ref[...].astype(F32)
    for n, (src, dst) in enumerate(((x_ref, gate_ref), (x_ref, up_ref), (g_ref, down_ref))):
        part = lhs[:, n * rows : (n + 1) * rows].reshape(pieces * rows, slots).astype(BF16)
        dst[...] = jnp.dot(part, src[...], preferred_element_type=F32).astype(BF16)


def weight_grads(lhs, x, g):
    pieces, stacked, slots = lhs.shape
    features = x.shape[1]
    rows = stacked // 3
    tile = features // 8
    ispec = pl.BlockSpec((slots, tile), lambda i: (0, i))
    ospec = pl.BlockSpec((pieces * rows, tile), lambda i: (0, i))
    oshape = jax.ShapeDtypeStruct((pieces * rows, features), BF16)
    return pl.pallas_call(
        weights_kernel,
        grid=(features // tile,),
        in_specs=[pl.BlockSpec((pieces, stacked, slots), lambda i: (0, 0, 0)), ispec, ispec],
        out_specs=[ospec] * 3,
        out_shape=[oshape] * 3,
        compiler_params=PARAMS,
        cost_estimate=pl.CostEstimate(
            flops=6 * slots * features * pieces * rows,
            bytes_accessed=16 * 1024 * 1024,
            transcendentals=0,
        ),
        name="weight_grads",
    )(lhs, x, g)


def route_places(ids, probs, expert, wide):
    named = ids == expert
    mine = jnp.any(named, axis=2)
    weight = jnp.sum(jnp.where(named, probs, 0.0), axis=2)
    blocks, tokens = mine.shape
    earlier = jnp.arange(tokens)[:, None] < jnp.arange(tokens)[None, :]
    slot = jnp.sum(mine[:, :, None] & earlier[None], axis=1)
    block = jnp.arange(blocks)
    column, branch = block % wide, block // wide
    turned = column % SIDE * SIDE + column // SIDE
    group = jnp.where(expert % 2 == 0, column, turned)
    start = (group * (blocks // wide) + branch) * CAP
    place = jnp.where(mine, start[:, None] + slot, -1)
    return place.astype(jnp.int32).reshape(1, blocks * tokens), weight


def stage_groups(experts, wide, odd):
    groups = []
    for branch in range(experts):
        for k in range(SIDE):
            fast = branch % 2 != odd
            members = [k * SIDE + n if fast else n * SIDE + k for n in range(SIDE)]
            groups.append([branch * wide + m for m in members])
    return groups


def exchange(value, axis):
    return lax.all_to_all(value, axis, split_axis=0, concat_axis=0, tiled=True)


def on_device(x_tokens, out_grad, expert_ids, gate_probs, w_gate, w_up, w_down, attn_out):
    experts = lax.axis_size("branch")
    wide = lax.axis_size("wide")
    blocks = experts * wide
    tokens, features = x_tokens.shape
    both = ("branch", "wide")
    branch_index = lax.axis_index("branch")
    wide_index = lax.axis_index("wide")

    gathered = lax.all_gather(
        jnp.concatenate([x_tokens, out_grad], axis=0), both, axis=0, tiled=True
    )
    gathered = gathered.reshape(blocks, 2 * tokens, features)

    meta = jnp.concatenate([expert_ids.astype(F32), gate_probs], axis=1)
    meta = jnp.pad(meta, ((0, 0), (0, 124)))
    meta = exchange(jnp.broadcast_to(meta[None], (blocks,) + meta.shape), both)
    ids = meta[:, :, 0:2].astype(jnp.int32)
    probs = meta[:, :, 2:4]
    place, weight = route_places(ids, probs, branch_index, wide)
    other_place, _ = route_places(ids, probs, wide_index // (wide // experts), wide)

    scaled = (attn_out[0].astype(F32) * (1.0 / experts)).astype(BF16)
    gathered, scaled = lax.optimization_barrier((gathered, scaled))

    send, back = expert(
        place, weight.reshape(1, -1), gathered, w_gate[0], w_up[0], w_down[0], wide
    )

    spread = lax.all_gather(send, "branch", axis=0, tiled=True)
    xe, ge = pick_rows(other_place, gathered)
    spread, scaled, xe, ge = lax.optimization_barrier((spread, scaled, xe, ge))
    spread = spread.reshape((experts, wide) + send.shape[1:])
    copies = wide // experts
    mine = lax.dynamic_slice_in_dim(spread, branch_index * copies, copies, 1)
    merged_attn = lax.psum_scatter(scaled, "branch", scatter_dimension=0, tiled=True)

    first = lax.all_to_all(
        back,
        both,
        split_axis=0,
        concat_axis=0,
        axis_index_groups=stage_groups(experts, wide, 0),
        tiled=True,
    )
    first, mine = lax.optimization_barrier((first, mine.reshape(send.shape)))
    relayed = exchange(mine, "wide")
    position = jnp.where(branch_index % 2 == 0, wide_index % SIDE, wide_index // SIDE)
    sums = first_sum(
        position.astype(jnp.int32).reshape(1), first.reshape((SIDE, SIDE) + back.shape[1:])
    )
    second = [sums[0]]
    for distance in range(1, SIDE):
        pairs = [
            (group[n], group[(n + distance) % SIDE])
            for group in stage_groups(experts, wide, 1)
            for n in range(SIDE)
        ]
        second.append(lax.ppermute(sums[distance], both, pairs))
    returned = gather_blocks(second, experts)
    grad_gate, grad_up, grad_down = weight_grads(relayed, xe, ge)
    got = exchange(returned, "branch")

    named = jnp.any(expert_ids[None] == jnp.arange(experts)[:, None, None], axis=2)
    earlier = jnp.arange(tokens)[:, None] < jnp.arange(tokens)[None, :]
    slot = jnp.sum(named[:, :, None] & earlier[None], axis=1)
    chosen = named[:, :, None] & (slot[:, :, None] == jnp.arange(CAP)[None, None, :])
    mixed, token_grad = combine(chosen.astype(F32), got)

    layout = (1, 1, wide, w_gate.shape[1] // wide, features)
    return (
        mixed,
        token_grad,
        merged_attn,
        grad_gate.reshape(layout),
        grad_up.reshape(layout),
        grad_down.reshape(layout),
    )


def solution(mesh):
    in_specs = (
        P(("branch", "wide"), None),
        P(("branch", "wide"), None),
        P(("branch", "wide"), None),
        P(("branch", "wide"), None),
        P("branch", "wide", None),
        P("branch", "wide", None),
        P("branch", "wide", None),
        P("branch", None, "wide"),
    )
    out_specs = (
        P(("branch", "wide"), None),
        P(("branch", "wide"), None),
        P("branch", "wide"),
        P("wide", "branch", None, None, None),
        P("wide", "branch", None, None, None),
        P("wide", "branch", None, None, None),
    )
    return jax.shard_map(
        on_device, mesh=mesh, in_specs=in_specs, out_specs=out_specs, check_vma=False
    )
```

```python
import functools

import jax
import jax.numpy as jnp
from jax import lax
from jax.experimental import pallas as pl
from jax.experimental.pallas import tpu as pltpu
from jax.sharding import PartitionSpec as P

F32 = jnp.float32
BF16 = jnp.bfloat16
CAP = 3
SIDE = 4
LAST = (((1,), (1,)), ((), ()))
PARAMS = pltpu.CompilerParams(vmem_limit_bytes=58 * 1024 * 1024)


SMALL = pltpu.CompilerParams(vmem_limit_bytes=16 * 1024 * 1024)


def split_rows(rows_ref):
    blocks, per_block, lanes = rows_ref.shape
    half = per_block // 2
    rows = rows_ref[...]
    x = rows[:, :half].reshape(blocks * half, lanes)
    g = rows[:, half:].reshape(blocks * half, lanes)
    return x, g


def one_hot_rows(place, count):
    row = lax.broadcasted_iota(jnp.int32, (count, place.shape[1]), 0)
    return jnp.where(row == place, 1.0, 0.0).astype(BF16)


def expert_kernel(
    position_ref, place_ref, prob_ref, rows_ref, wg_ref, wu_ref, wd_ref, send_ref, *refs, steps
):
    back_refs, (pair_acc, hg_acc, flat, acts, kept) = refs[:-5], refs[-5:]
    step = pl.program_id(0)
    slots = acts.shape[1]
    chunk = slots // len(back_refs)

    @pl.when(step < steps)
    def _():
        x, g = split_rows(rows_ref)
        for n, w_ref in enumerate((wg_ref, wu_ref, wd_ref)):
            kept[step, n] = w_ref[...]
        pair = jnp.concatenate([wg_ref[...], wu_ref[...]], axis=0)
        for acc, w, rhs in ((pair_acc, pair, x), (hg_acc, wd_ref[...], g)):
            part = lax.dot_general(w, rhs, LAST, preferred_element_type=F32)

            @pl.when(step == 0)
            def _(acc=acc, part=part):
                acc[...] = part

            @pl.when(step > 0)
            def _(acc=acc, part=part):
                acc[...] += part

    @pl.when(step == steps)
    def _():
        prob = prob_ref[...]
        hidden = hg_acc.shape[0]
        gate = pair_acc[:hidden]
        up = pair_acc[hidden:]
        sig = jax.nn.sigmoid(gate)
        back = hg_acc[...] * prob
        gate_sig = gate * sig
        pick = one_hot_rows(place_ref[...], slots)
        values = (
            back * up * sig * (1.0 + gate * (1.0 - sig)),
            back * gate_sig,
            gate_sig * up * prob,
        )
        pieces, stacked, _ = send_ref.shape
        height = stacked // 3
        turned = []
        for n, value in enumerate(values):
            got = lax.dot_general(value.astype(BF16), pick, LAST, preferred_element_type=F32)
            flat[...] = got.T.astype(BF16)
            for distance in range(len(back_refs)):
                member = lax.rem(position_ref[0] + distance, len(back_refs))
                rows = pl.ds(pl.multiple_of(member * chunk, chunk), chunk)
                acts[n, distance * chunk : (distance + 1) * chunk] = flat[rows]
            turned.append(got.reshape(pieces, height, slots))
        send_ref[...] = jnp.concatenate(turned, axis=1).astype(BF16)

    @pl.when(step >= steps)
    def _():
        tile = step - steps
        out = jnp.dot(acts[2], kept[tile, 2], preferred_element_type=F32)
        grad = jnp.dot(acts[0], kept[tile, 0], preferred_element_type=F32) + jnp.dot(
            acts[1], kept[tile, 1], preferred_element_type=F32
        )
        for distance, ref in enumerate(back_refs):
            count, _, height, width = ref.shape
            for o, value in enumerate((out, grad)):
                part = value[distance * chunk : (distance + 1) * chunk]
                ref[:, o] = part.reshape(count, height, width).astype(BF16)


def expert(position, place, prob, rows, wg, wu, wd, pieces):
    blocks, per_block, features = rows.shape
    hidden = wg.shape[0]
    slots = blocks * CAP
    tokens = place.shape[1]
    steps = 4
    tile = features // steps
    wspec = pl.BlockSpec((hidden, tile), lambda i: (0, jnp.minimum(i, steps - 1)))
    line = pl.BlockSpec((1, tokens), lambda i: (0, 0))
    stacked = 3 * hidden // pieces
    return pl.pallas_call(
        functools.partial(expert_kernel, steps=steps),
        grid=(2 * steps,),
        in_specs=[
            pl.BlockSpec(memory_space=pltpu.SMEM), line, line,
            pl.BlockSpec((blocks, per_block, tile), lambda i: (0, 0, jnp.minimum(i, steps - 1))),
            wspec, wspec, wspec,
        ],
        out_specs=[
            pl.BlockSpec((pieces, stacked, slots), lambda i: (0, 0, 0)),
        ]
        + [
            pl.BlockSpec(
                (pieces // SIDE, 2, slots // pieces, tile),
                lambda i: (0, 0, 0, jnp.maximum(i - steps, 0)),
            )
        ]
        * SIDE,
        out_shape=[
            jax.ShapeDtypeStruct((pieces, stacked, slots), BF16),
        ]
        + [jax.ShapeDtypeStruct((pieces // SIDE, 2, slots // pieces, features), BF16)] * SIDE,
        scratch_shapes=[
            pltpu.VMEM((2 * hidden, tokens), F32),
            pltpu.VMEM((hidden, tokens), F32),
            pltpu.VMEM((slots, hidden), BF16),
            pltpu.VMEM((3, slots, hidden), BF16),
            pltpu.VMEM((steps, 3, hidden, tile), BF16),
        ],
        compiler_params=PARAMS,
        cost_estimate=pl.CostEstimate(
            flops=6 * tokens * features * hidden,
            bytes_accessed=33 * 1024 * 1024,
            transcendentals=tokens * hidden,
        ),
        name="expert",
    )(position, place, prob, rows, wg, wu, wd)


def pick_kernel(place_ref, rows_ref, x_ref, g_ref):
    x, g = split_rows(rows_ref)
    pick = one_hot_rows(place_ref[...], x_ref.shape[0])
    x_ref[...] = jnp.dot(pick, x, preferred_element_type=F32).astype(BF16)
    g_ref[...] = jnp.dot(pick, g, preferred_element_type=F32).astype(BF16)


def pick_rows(place, rows):
    blocks, per_block, features = rows.shape
    slots = blocks * CAP
    tokens = place.shape[1]
    steps = 4
    tile = features // steps
    spec = pl.BlockSpec((slots, tile), lambda i: (0, i))
    return pl.pallas_call(
        pick_kernel,
        grid=(steps,),
        in_specs=[
            pl.BlockSpec((1, tokens), lambda i: (0, 0)),
            pl.BlockSpec((blocks, per_block, tile), lambda i: (0, 0, i)),
        ],
        out_specs=[spec, spec],
        out_shape=[jax.ShapeDtypeStruct((slots, features), BF16)] * 2,
        compiler_params=PARAMS,
        cost_estimate=pl.CostEstimate(
            flops=4 * slots * tokens * features, bytes_accessed=24 * 1024 * 1024, transcendentals=0
        ),
        name="pick_rows",
    )(place, rows)


def first_sum_kernel(position_ref, *refs):
    half = len(refs) // 2
    total, outs = refs[-1], refs[half:-1]
    total[...] = sum(ref[...].astype(F32) for ref in refs[:half])
    for distance, ref in enumerate(outs):
        ref[...] = total[lax.rem(position_ref[0] + distance, len(outs))].astype(BF16)


def first_sum(position, got):
    parts, _, height, features = got[0].shape
    steps = 4
    tile = features // steps
    return pl.pallas_call(
        first_sum_kernel,
        grid=(steps,),
        in_specs=[
            pl.BlockSpec(memory_space=pltpu.SMEM),
        ]
        + [pl.BlockSpec((parts, 2, height, tile), lambda i: (0, 0, 0, i))] * parts,
        out_specs=[pl.BlockSpec((2, height, tile), lambda i: (0, 0, i))] * parts,
        out_shape=[jax.ShapeDtypeStruct((2, height, features), BF16)] * parts,
        scratch_shapes=[pltpu.VMEM((parts, 2, height, tile), F32)],
        compiler_params=SMALL,
        name="first_sum",
    )(position, *got)


def gather_kernel(*refs):
    ret_ref = refs[-1]
    total = sum(ref[...].astype(F32) for ref in refs[:-1])
    experts, padded, tile = ret_ref.shape
    blank = jnp.zeros((padded // 2 - CAP, tile), F32)
    for block in range(experts):
        rows = []
        for o in range(2):
            rows += [total[o, block * CAP : (block + 1) * CAP], blank]
        ret_ref[block] = jnp.concatenate(rows, axis=0).astype(BF16)


def gather_blocks(got, experts):
    _, height, features = got[0].shape
    steps = 4
    tile = features // steps
    return pl.pallas_call(
        gather_kernel,
        grid=(steps,),
        in_specs=[pl.BlockSpec((2, height, tile), lambda i: (0, 0, i))] * len(got),
        out_specs=pl.BlockSpec((experts, 8, tile), lambda i: (0, 0, i)),
        out_shape=jax.ShapeDtypeStruct((experts, 8, features), BF16),
        compiler_params=SMALL,
        name="gather_blocks",
    )(*got)


def combine_kernel(chosen_ref, got_ref, mixed_ref, grad_ref):
    experts = got_ref.shape[0]
    for o, ref in enumerate((mixed_ref, grad_ref)):
        total = jnp.zeros(ref.shape, F32)
        for e in range(experts):
            rows = got_ref[e].astype(F32)
            chosen = chosen_ref[e]
            for s in range(CAP):
                total = total + chosen[:, s : s + 1] * rows[4 * o + s : 4 * o + s + 1]
        ref[...] = total.astype(BF16)


def combine(chosen, got):
    experts, padded, features = got.shape
    tokens = chosen.shape[1]
    steps = 2
    tile = features // steps
    spec = pl.BlockSpec((tokens, tile), lambda i: (0, i))
    return pl.pallas_call(
        combine_kernel,
        grid=(steps,),
        in_specs=[
            pl.BlockSpec((experts, tokens, CAP), lambda i: (0, 0, 0)),
            pl.BlockSpec((experts, padded, tile), lambda i: (0, 0, i)),
        ],
        out_specs=[spec, spec],
        out_shape=[jax.ShapeDtypeStruct((tokens, features), BF16)] * 2,
        compiler_params=SMALL,
        name="combine",
    )(chosen, got)


def weights_kernel(lhs_ref, x_ref, g_ref, gate_ref, up_ref, down_ref):
    pieces, stacked, slots = lhs_ref.shape
    rows = stacked // 3
    lhs = lhs_ref[...].astype(F32)
    for n, (src, dst) in enumerate(((x_ref, gate_ref), (x_ref, up_ref), (g_ref, down_ref))):
        part = lhs[:, n * rows : (n + 1) * rows].reshape(pieces * rows, slots).astype(BF16)
        dst[...] = jnp.dot(part, src[...], preferred_element_type=F32).astype(BF16)


def weight_grads(lhs, x, g):
    pieces, stacked, slots = lhs.shape
    features = x.shape[1]
    rows = stacked // 3
    tile = features // 8
    ispec = pl.BlockSpec((slots, tile), lambda i: (0, i))
    ospec = pl.BlockSpec((pieces * rows, tile), lambda i: (0, i))
    oshape = jax.ShapeDtypeStruct((pieces * rows, features), BF16)
    return pl.pallas_call(
        weights_kernel,
        grid=(features // tile,),
        in_specs=[pl.BlockSpec((pieces, stacked, slots), lambda i: (0, 0, 0)), ispec, ispec],
        out_specs=[ospec] * 3,
        out_shape=[oshape] * 3,
        compiler_params=PARAMS,
        cost_estimate=pl.CostEstimate(
            flops=6 * slots * features * pieces * rows,
            bytes_accessed=16 * 1024 * 1024,
            transcendentals=0,
        ),
        name="weight_grads",
    )(lhs, x, g)


def route_places(ids, probs, expert, wide):
    named = ids == expert
    mine = jnp.any(named, axis=2)
    weight = jnp.sum(jnp.where(named, probs, 0.0), axis=2)
    blocks, tokens = mine.shape
    earlier = jnp.arange(tokens)[:, None] < jnp.arange(tokens)[None, :]
    slot = jnp.sum(mine[:, :, None] & earlier[None], axis=1)
    block = jnp.arange(blocks)
    column, branch = block % wide, block // wide
    turned = column % SIDE * SIDE + column // SIDE
    group = jnp.where(expert % 2 == 0, column, turned)
    start = (group * (blocks // wide) + branch) * CAP
    place = jnp.where(mine, start[:, None] + slot, -1)
    return place.astype(jnp.int32).reshape(1, blocks * tokens), weight


def stage_groups(experts, wide, odd):
    groups = []
    for branch in range(experts):
        for k in range(SIDE):
            fast = branch % 2 != odd
            members = [k * SIDE + n if fast else n * SIDE + k for n in range(SIDE)]
            groups.append([branch * wide + m for m in members])
    return groups


def exchange(value, axis):
    return lax.all_to_all(value, axis, split_axis=0, concat_axis=0, tiled=True)


def on_device(x_tokens, out_grad, expert_ids, gate_probs, w_gate, w_up, w_down, attn_out):
    experts = lax.axis_size("branch")
    wide = lax.axis_size("wide")
    blocks = experts * wide
    tokens, features = x_tokens.shape
    both = ("branch", "wide")
    branch_index = lax.axis_index("branch")
    wide_index = lax.axis_index("wide")

    gathered = lax.all_gather(
        jnp.concatenate([x_tokens, out_grad], axis=0), both, axis=0, tiled=True
    )
    gathered = gathered.reshape(blocks, 2 * tokens, features)

    meta = jnp.concatenate([expert_ids.astype(F32), gate_probs], axis=1)
    meta = jnp.pad(meta, ((0, 0), (0, 124)))
    meta = exchange(jnp.broadcast_to(meta[None], (blocks,) + meta.shape), both)
    ids = meta[:, :, 0:2].astype(jnp.int32)
    probs = meta[:, :, 2:4]
    place, weight = route_places(ids, probs, branch_index, wide)
    other_place, _ = route_places(ids, probs, wide_index // (wide // experts), wide)

    scaled = (attn_out[0].astype(F32) * (1.0 / experts)).astype(BF16)
    gathered, scaled = lax.optimization_barrier((gathered, scaled))

    slow, fast = wide_index // SIDE, wide_index % SIDE
    even = branch_index % 2 == 0
    position_one = jnp.where(even, slow, fast).astype(jnp.int32).reshape(1)
    position_two = jnp.where(even, fast, slow).astype(jnp.int32).reshape(1)

    send, *chunks = expert(
        position_one,
        place,
        weight.reshape(1, -1),
        gathered,
        w_gate[0],
        w_up[0],
        w_down[0],
        wide,
    )

    def deliver(parts, odd):
        groups = stage_groups(experts, wide, odd)
        got = [parts[0]]
        for distance in range(1, SIDE):
            pairs = [(g[n], g[(n + distance) % SIDE]) for g in groups for n in range(SIDE)]
            got.append(lax.ppermute(parts[distance], both, pairs))
        return got

    first = deliver(chunks, 0)
    mine = exchange(send, "branch")
    xe, ge = pick_rows(other_place, gathered)
    first, mine, scaled, xe, ge = lax.optimization_barrier((first, mine, scaled, xe, ge))
    merged_attn = lax.psum_scatter(scaled, "branch", scatter_dimension=0, tiled=True)
    relayed = exchange(mine, "wide")
    second = deliver(first_sum(position_two, first), 1)
    returned = gather_blocks(second, experts)
    grad_gate, grad_up, grad_down = weight_grads(relayed, xe, ge)
    got = exchange(returned, "branch")

    named = jnp.any(expert_ids[None] == jnp.arange(experts)[:, None, None], axis=2)
    earlier = jnp.arange(tokens)[:, None] < jnp.arange(tokens)[None, :]
    slot = jnp.sum(named[:, :, None] & earlier[None], axis=1)
    chosen = named[:, :, None] & (slot[:, :, None] == jnp.arange(CAP)[None, None, :])
    mixed, token_grad = combine(chosen.astype(F32), got)

    layout = (1, 1, wide, w_gate.shape[1] // wide, features)
    return (
        mixed,
        token_grad,
        merged_attn,
        grad_gate.reshape(layout),
        grad_up.reshape(layout),
        grad_down.reshape(layout),
    )


def solution(mesh):
    in_specs = (
        P(("branch", "wide"), None),
        P(("branch", "wide"), None),
        P(("branch", "wide"), None),
        P(("branch", "wide"), None),
        P("branch", "wide", None),
        P("branch", "wide", None),
        P("branch", "wide", None),
        P("branch", None, "wide"),
    )
    out_specs = (
        P(("branch", "wide"), None),
        P(("branch", "wide"), None),
        P("branch", "wide"),
        P("wide", "branch", None, None, None),
        P("wide", "branch", None, None, None),
        P("wide", "branch", None, None, None),
    )
    return jax.shard_map(
        on_device, mesh=mesh, in_specs=in_specs, out_specs=out_specs, check_vma=False
    )
```

```python
import functools

import jax
import jax.numpy as jnp
from jax import lax
from jax.experimental import pallas as pl
from jax.experimental.pallas import tpu as pltpu
from jax.sharding import PartitionSpec as P

F32 = jnp.float32
BF16 = jnp.bfloat16
CAP = 3
SIDE = 4
LAST = (((1,), (1,)), ((), ()))
PARAMS = pltpu.CompilerParams(vmem_limit_bytes=58 * 1024 * 1024)


SMALL = pltpu.CompilerParams(vmem_limit_bytes=16 * 1024 * 1024)


def split_rows(rows_ref):
    blocks, per_block, lanes = rows_ref.shape
    half = per_block // 2
    rows = rows_ref[...]
    x = rows[:, :half].reshape(blocks * half, lanes)
    g = rows[:, half:].reshape(blocks * half, lanes)
    return x, g


def one_hot_rows(place, count):
    row = lax.broadcasted_iota(jnp.int32, (count, place.shape[1]), 0)
    return jnp.where(row == place, 1.0, 0.0).astype(BF16)


def expert_kernel(
    position_ref, place_ref, prob_ref, rows_ref, wg_ref, wu_ref, wd_ref, send_ref, *refs, steps
):
    back_refs, (pair_acc, hg_acc, flat, acts, kept) = refs[:-5], refs[-5:]
    step = pl.program_id(0)
    slots = acts.shape[1]
    chunk = slots // len(back_refs)

    @pl.when(step == 0)
    def _():
        pair_acc[...] = jnp.zeros_like(pair_acc)
        hg_acc[...] = jnp.zeros_like(hg_acc)

    @pl.when(step < steps)
    def _():
        x, g = split_rows(rows_ref)
        for n, w_ref in enumerate((wg_ref, wu_ref, wd_ref)):
            kept[step, n] = w_ref[...]
        pair = jnp.concatenate([wg_ref[...], wu_ref[...]], axis=0)
        for acc, w, rhs in ((pair_acc, pair, x), (hg_acc, wd_ref[...], g)):
            acc[...] += lax.dot_general(w, rhs, LAST, preferred_element_type=F32)

    @pl.when(step == steps)
    def _():
        prob = prob_ref[...]
        hidden = hg_acc.shape[0]
        gate = pair_acc[:hidden]
        up = pair_acc[hidden:]
        sig = jax.nn.sigmoid(gate)
        back = hg_acc[...] * prob
        gate_sig = gate * sig
        pick = one_hot_rows(place_ref[...], slots)
        values = (
            back * up * sig * (1.0 + gate * (1.0 - sig)),
            back * gate_sig,
            gate_sig * up * prob,
        )
        pieces, stacked, _ = send_ref.shape
        height = stacked // 3
        turned = []
        for n, value in enumerate(values):
            got = lax.dot_general(value.astype(BF16), pick, LAST, preferred_element_type=F32)
            flat[...] = got.T.astype(BF16)
            for distance in range(len(back_refs)):
                member = lax.rem(position_ref[0] + distance, len(back_refs))
                rows = pl.ds(pl.multiple_of(member * chunk, chunk), chunk)
                acts[n, distance * chunk : (distance + 1) * chunk] = flat[rows]
            turned.append(got.reshape(pieces, height, slots))
        send_ref[...] = jnp.concatenate(turned, axis=1).astype(BF16)

    @pl.when(step >= steps)
    def _():
        tile = step - steps
        out = jnp.dot(acts[2], kept[tile, 2], preferred_element_type=F32)
        grad = jnp.dot(acts[0], kept[tile, 0], preferred_element_type=F32) + jnp.dot(
            acts[1], kept[tile, 1], preferred_element_type=F32
        )
        for distance, ref in enumerate(back_refs):
            count, _, height, width = ref.shape
            for o, value in enumerate((out, grad)):
                part = value[distance * chunk : (distance + 1) * chunk]
                ref[:, o] = part.reshape(count, height, width).astype(BF16)


def expert(position, place, prob, rows, wg, wu, wd, pieces):
    blocks, per_block, features = rows.shape
    hidden = wg.shape[0]
    slots = blocks * CAP
    tokens = place.shape[1]
    steps = 4
    tile = features // steps
    wspec = pl.BlockSpec((hidden, tile), lambda i: (0, jnp.minimum(i, steps - 1)))
    line = pl.BlockSpec((1, tokens), lambda i: (0, 0))
    stacked = 3 * hidden // pieces
    return pl.pallas_call(
        functools.partial(expert_kernel, steps=steps),
        grid=(2 * steps,),
        in_specs=[
            pl.BlockSpec(memory_space=pltpu.SMEM), line, line,
            pl.BlockSpec((blocks, per_block, tile), lambda i: (0, 0, jnp.minimum(i, steps - 1))),
            wspec, wspec, wspec,
        ],
        out_specs=[
            pl.BlockSpec((pieces, stacked, slots), lambda i: (0, 0, 0)),
        ]
        + [
            pl.BlockSpec(
                (pieces // SIDE, 2, slots // pieces, tile),
                lambda i: (0, 0, 0, jnp.maximum(i - steps, 0)),
            )
        ]
        * SIDE,
        out_shape=[
            jax.ShapeDtypeStruct((pieces, stacked, slots), BF16),
        ]
        + [jax.ShapeDtypeStruct((pieces // SIDE, 2, slots // pieces, features), BF16)] * SIDE,
        scratch_shapes=[
            pltpu.VMEM((2 * hidden, tokens), F32),
            pltpu.VMEM((hidden, tokens), F32),
            pltpu.VMEM((slots, hidden), BF16),
            pltpu.VMEM((3, slots, hidden), BF16),
            pltpu.VMEM((steps, 3, hidden, tile), BF16),
        ],
        compiler_params=PARAMS,
        cost_estimate=pl.CostEstimate(
            flops=6 * tokens * features * hidden,
            bytes_accessed=33 * 1024 * 1024,
            transcendentals=tokens * hidden,
        ),
        name="expert",
    )(position, place, prob, rows, wg, wu, wd)


def pick_kernel(place_ref, rows_ref, x_ref, g_ref):
    x, g = split_rows(rows_ref)
    pick = one_hot_rows(place_ref[...], x_ref.shape[0])
    x_ref[...] = jnp.dot(pick, x, preferred_element_type=F32).astype(BF16)
    g_ref[...] = jnp.dot(pick, g, preferred_element_type=F32).astype(BF16)


def pick_rows(place, rows):
    blocks, per_block, features = rows.shape
    slots = blocks * CAP
    tokens = place.shape[1]
    steps = 4
    tile = features // steps
    spec = pl.BlockSpec((slots, tile), lambda i: (0, i))
    return pl.pallas_call(
        pick_kernel,
        grid=(steps,),
        in_specs=[
            pl.BlockSpec((1, tokens), lambda i: (0, 0)),
            pl.BlockSpec((blocks, per_block, tile), lambda i: (0, 0, i)),
        ],
        out_specs=[spec, spec],
        out_shape=[jax.ShapeDtypeStruct((slots, features), BF16)] * 2,
        compiler_params=PARAMS,
        cost_estimate=pl.CostEstimate(
            flops=4 * slots * tokens * features, bytes_accessed=24 * 1024 * 1024, transcendentals=0
        ),
        name="pick_rows",
    )(place, rows)


def first_sum_kernel(position_ref, *refs):
    half = len(refs) // 2
    total, outs = refs[-1], refs[half:-1]
    total[...] = sum(ref[...].astype(F32) for ref in refs[:half])
    for distance, ref in enumerate(outs):
        ref[...] = total[lax.rem(position_ref[0] + distance, len(outs))].astype(BF16)


def first_sum(position, got):
    parts, _, height, features = got[0].shape
    steps = 4
    tile = features // steps
    return pl.pallas_call(
        first_sum_kernel,
        grid=(steps,),
        in_specs=[
            pl.BlockSpec(memory_space=pltpu.SMEM),
        ]
        + [pl.BlockSpec((parts, 2, height, tile), lambda i: (0, 0, 0, i))] * parts,
        out_specs=[pl.BlockSpec((2, height, tile), lambda i: (0, 0, i))] * parts,
        out_shape=[jax.ShapeDtypeStruct((2, height, features), BF16)] * parts,
        scratch_shapes=[pltpu.VMEM((parts, 2, height, tile), F32)],
        compiler_params=SMALL,
        name="first_sum",
    )(position, *got)


def gather_kernel(*refs):
    ret_ref = refs[-1]
    total = sum(ref[...].astype(F32) for ref in refs[:-1])
    experts, padded, tile = ret_ref.shape
    blank = jnp.zeros((padded // 2 - CAP, tile), F32)
    for block in range(experts):
        rows = []
        for o in range(2):
            rows += [total[o, block * CAP : (block + 1) * CAP], blank]
        ret_ref[block] = jnp.concatenate(rows, axis=0).astype(BF16)


def gather_blocks(got, experts):
    _, height, features = got[0].shape
    steps = 4
    tile = features // steps
    return pl.pallas_call(
        gather_kernel,
        grid=(steps,),
        in_specs=[pl.BlockSpec((2, height, tile), lambda i: (0, 0, i))] * len(got),
        out_specs=pl.BlockSpec((experts, 8, tile), lambda i: (0, 0, i)),
        out_shape=jax.ShapeDtypeStruct((experts, 8, features), BF16),
        compiler_params=SMALL,
        name="gather_blocks",
    )(*got)


def combine_kernel(chosen_ref, got_ref, mixed_ref, grad_ref):
    experts = got_ref.shape[0]
    for o, ref in enumerate((mixed_ref, grad_ref)):
        total = jnp.zeros(ref.shape, F32)
        for e in range(experts):
            rows = got_ref[e].astype(F32)
            chosen = chosen_ref[e]
            for s in range(CAP):
                total = total + chosen[:, s : s + 1] * rows[4 * o + s : 4 * o + s + 1]
        ref[...] = total.astype(BF16)


def combine(chosen, got):
    experts, padded, features = got.shape
    tokens = chosen.shape[1]
    steps = 2
    tile = features // steps
    spec = pl.BlockSpec((tokens, tile), lambda i: (0, i))
    return pl.pallas_call(
        combine_kernel,
        grid=(steps,),
        in_specs=[
            pl.BlockSpec((experts, tokens, CAP), lambda i: (0, 0, 0)),
            pl.BlockSpec((experts, padded, tile), lambda i: (0, 0, i)),
        ],
        out_specs=[spec, spec],
        out_shape=[jax.ShapeDtypeStruct((tokens, features), BF16)] * 2,
        compiler_params=SMALL,
        name="combine",
    )(chosen, got)


def weights_kernel(lhs_ref, x_ref, g_ref, gate_ref, up_ref, down_ref):
    pieces, stacked, slots = lhs_ref.shape
    rows = stacked // 3
    lhs = lhs_ref[...].astype(F32)
    for n, (src, dst) in enumerate(((x_ref, gate_ref), (x_ref, up_ref), (g_ref, down_ref))):
        part = lhs[:, n * rows : (n + 1) * rows].reshape(pieces * rows, slots).astype(BF16)
        dst[...] = jnp.dot(part, src[...], preferred_element_type=F32).astype(BF16)


def weight_grads(lhs, x, g):
    pieces, stacked, slots = lhs.shape
    features = x.shape[1]
    rows = stacked // 3
    tile = features // 8
    ispec = pl.BlockSpec((slots, tile), lambda i: (0, i))
    ospec = pl.BlockSpec((pieces * rows, tile), lambda i: (0, i))
    oshape = jax.ShapeDtypeStruct((pieces * rows, features), BF16)
    return pl.pallas_call(
        weights_kernel,
        grid=(features // tile,),
        in_specs=[pl.BlockSpec((pieces, stacked, slots), lambda i: (0, 0, 0)), ispec, ispec],
        out_specs=[ospec] * 3,
        out_shape=[oshape] * 3,
        compiler_params=PARAMS,
        cost_estimate=pl.CostEstimate(
            flops=6 * slots * features * pieces * rows,
            bytes_accessed=16 * 1024 * 1024,
            transcendentals=0,
        ),
        name="weight_grads",
    )(lhs, x, g)


def route_places(ids, probs, expert, wide):
    named = ids == expert
    mine = jnp.any(named, axis=2)
    weight = jnp.sum(jnp.where(named, probs, 0.0), axis=2)
    blocks, tokens = mine.shape
    earlier = jnp.arange(tokens)[:, None] < jnp.arange(tokens)[None, :]
    slot = jnp.sum(mine[:, :, None] & earlier[None], axis=1)
    block = jnp.arange(blocks)
    column, branch = block % wide, block // wide
    turned = column % SIDE * SIDE + column // SIDE
    group = jnp.where(expert % 2 == 0, column, turned)
    start = (group * (blocks // wide) + branch) * CAP
    place = jnp.where(mine, start[:, None] + slot, -1)
    return place.astype(jnp.int32).reshape(1, blocks * tokens), weight


def stage_groups(experts, wide, odd):
    groups = []
    for branch in range(experts):
        for k in range(SIDE):
            fast = branch % 2 != odd
            members = [k * SIDE + n if fast else n * SIDE + k for n in range(SIDE)]
            groups.append([branch * wide + m for m in members])
    return groups


def exchange(value, axis):
    return lax.all_to_all(value, axis, split_axis=0, concat_axis=0, tiled=True)


def on_device(x_tokens, out_grad, expert_ids, gate_probs, w_gate, w_up, w_down, attn_out):
    experts = lax.axis_size("branch")
    wide = lax.axis_size("wide")
    blocks = experts * wide
    tokens, features = x_tokens.shape
    both = ("branch", "wide")
    branch_index = lax.axis_index("branch")
    wide_index = lax.axis_index("wide")

    gathered = lax.all_gather(
        jnp.concatenate([x_tokens, out_grad], axis=0), both, axis=0, tiled=True
    )
    gathered = gathered.reshape(blocks, 2 * tokens, features)

    meta = jnp.concatenate([expert_ids.astype(F32), gate_probs], axis=1)
    meta = jnp.pad(meta, ((0, 0), (0, 124)))
    meta = exchange(jnp.broadcast_to(meta[None], (blocks,) + meta.shape), both)
    ids = meta[:, :, 0:2].astype(jnp.int32)
    probs = meta[:, :, 2:4]
    place, weight = route_places(ids, probs, branch_index, wide)
    other_place, _ = route_places(ids, probs, wide_index // (wide // experts), wide)

    scaled = (attn_out[0].astype(F32) * (1.0 / experts)).astype(BF16)
    gathered, scaled = lax.optimization_barrier((gathered, scaled))

    slow, fast = wide_index // SIDE, wide_index % SIDE
    even = branch_index % 2 == 0
    position_one = jnp.where(even, slow, fast).astype(jnp.int32).reshape(1)
    position_two = jnp.where(even, fast, slow).astype(jnp.int32).reshape(1)

    send, *chunks = expert(
        position_one,
        place,
        weight.reshape(1, -1),
        gathered,
        w_gate[0],
        w_up[0],
        w_down[0],
        wide,
    )

    def deliver(parts, odd):
        groups = stage_groups(experts, wide, odd)
        got = [parts[0]]
        for distance in range(1, SIDE):
            pairs = [(g[n], g[(n + distance) % SIDE]) for g in groups for n in range(SIDE)]
            got.append(lax.ppermute(parts[distance], both, pairs))
        return got

    first = deliver(chunks, 0)
    mine = exchange(send, "branch")
    xe, ge = pick_rows(other_place, gathered)
    first, mine, scaled, xe, ge = lax.optimization_barrier((first, mine, scaled, xe, ge))
    merged_attn = lax.psum_scatter(scaled, "branch", scatter_dimension=0, tiled=True)
    relayed = exchange(mine, "wide")
    second = deliver(first_sum(position_two, first), 1)
    returned = gather_blocks(second, experts)
    grad_gate, grad_up, grad_down = weight_grads(relayed, xe, ge)
    got = exchange(returned, "branch")

    named = jnp.any(expert_ids[None] == jnp.arange(experts)[:, None, None], axis=2)
    earlier = jnp.arange(tokens)[:, None] < jnp.arange(tokens)[None, :]
    slot = jnp.sum(named[:, :, None] & earlier[None], axis=1)
    chosen = named[:, :, None] & (slot[:, :, None] == jnp.arange(CAP)[None, None, :])
    mixed, token_grad = combine(chosen.astype(F32), got)

    layout = (1, 1, wide, w_gate.shape[1] // wide, features)
    return (
        mixed,
        token_grad,
        merged_attn,
        grad_gate.reshape(layout),
        grad_up.reshape(layout),
        grad_down.reshape(layout),
    )


def solution(mesh):
    in_specs = (
        P(("branch", "wide"), None),
        P(("branch", "wide"), None),
        P(("branch", "wide"), None),
        P(("branch", "wide"), None),
        P("branch", "wide", None),
        P("branch", "wide", None),
        P("branch", "wide", None),
        P("branch", None, "wide"),
    )
    out_specs = (
        P(("branch", "wide"), None),
        P(("branch", "wide"), None),
        P("branch", "wide"),
        P("wide", "branch", None, None, None),
        P("wide", "branch", None, None, None),
        P("wide", "branch", None, None, None),
    )
    return jax.shard_map(
        on_device, mesh=mesh, in_specs=in_specs, out_specs=out_specs, check_vma=False
    )
```

```python
import functools

import jax
import jax.numpy as jnp
from jax import lax
from jax.experimental import pallas as pl
from jax.experimental.pallas import tpu as pltpu
from jax.sharding import PartitionSpec as P

F32 = jnp.float32
BF16 = jnp.bfloat16
CAP = 3
SIDE = 4
LAST = (((1,), (1,)), ((), ()))
PARAMS = pltpu.CompilerParams(vmem_limit_bytes=58 * 1024 * 1024)


SMALL = pltpu.CompilerParams(vmem_limit_bytes=16 * 1024 * 1024)


def split_rows(rows_ref):
    blocks, per_block, lanes = rows_ref.shape
    half = per_block // 2
    rows = rows_ref[...]
    x = rows[:, :half].reshape(blocks * half, lanes)
    g = rows[:, half:].reshape(blocks * half, lanes)
    return x, g


def one_hot_rows(place, count):
    row = lax.broadcasted_iota(jnp.int32, (count, place.shape[1]), 0)
    return jnp.where(row == place, 1.0, 0.0).astype(BF16)


def expert_kernel(
    position_ref, place_ref, prob_ref, rows_ref, wg_ref, wu_ref, wd_ref, send_ref, *refs, steps
):
    back_refs, (pair_acc, hg_acc, flat, acts, kept) = refs[:-5], refs[-5:]
    step = pl.program_id(0)
    slots = acts.shape[1]
    chunk = slots // len(back_refs)

    @pl.when(step == 0)
    def _():
        pair_acc[...] = jnp.zeros_like(pair_acc)
        hg_acc[...] = jnp.zeros_like(hg_acc)

    @pl.when(step < steps)
    def _():
        x, g = split_rows(rows_ref)
        for n, w_ref in enumerate((wg_ref, wu_ref, wd_ref)):
            kept[step, n] = w_ref[...]
        pair = jnp.concatenate([wg_ref[...], wu_ref[...]], axis=0)
        for acc, w, rhs in ((pair_acc, pair, x), (hg_acc, wd_ref[...], g)):
            acc[...] += lax.dot_general(w, rhs, LAST, preferred_element_type=F32)

    @pl.when(step == steps)
    def _():
        prob = prob_ref[...]
        hidden = hg_acc.shape[0]
        gate = pair_acc[:hidden]
        up = pair_acc[hidden:]
        sig = jax.nn.sigmoid(gate)
        back = hg_acc[...] * prob
        gate_sig = gate * sig
        pick = one_hot_rows(place_ref[...], slots)
        values = (
            back * up * sig * (1.0 + gate * (1.0 - sig)),
            back * gate_sig,
            gate_sig * up * prob,
        )
        pieces, stacked, _ = send_ref.shape
        height = stacked // 3
        turned = []
        for n, value in enumerate(values):
            got = lax.dot_general(value.astype(BF16), pick, LAST, preferred_element_type=F32)
            flat[...] = got.T.astype(BF16)
            for distance in range(len(back_refs)):
                member = lax.rem(position_ref[0] + distance, len(back_refs))
                rows = pl.ds(pl.multiple_of(member * chunk, chunk), chunk)
                acts[n, distance * chunk : (distance + 1) * chunk] = flat[rows]
            turned.append(got.reshape(pieces, height, slots))
        send_ref[...] = jnp.concatenate(turned, axis=1).astype(BF16)

    @pl.when(step >= steps)
    def _():
        tile = step - steps
        out = jnp.dot(acts[2], kept[tile, 2], preferred_element_type=F32)
        grad = jnp.dot(acts[0], kept[tile, 0], preferred_element_type=F32) + jnp.dot(
            acts[1], kept[tile, 1], preferred_element_type=F32
        )
        for distance, ref in enumerate(back_refs):
            count, _, height, width = ref.shape
            for o, value in enumerate((out, grad)):
                part = value[distance * chunk : (distance + 1) * chunk]
                ref[:, o] = part.reshape(count, height, width).astype(BF16)


def expert(position, place, prob, rows, wg, wu, wd, pieces):
    blocks, per_block, features = rows.shape
    hidden = wg.shape[0]
    slots = blocks * CAP
    tokens = place.shape[1]
    steps = 4
    tile = features // steps
    wspec = pl.BlockSpec((hidden, tile), lambda i: (0, jnp.minimum(i, steps - 1)))
    line = pl.BlockSpec((1, tokens), lambda i: (0, 0))
    stacked = 3 * hidden // pieces
    return pl.pallas_call(
        functools.partial(expert_kernel, steps=steps),
        grid=(2 * steps,),
        in_specs=[
            pl.BlockSpec(memory_space=pltpu.SMEM), line, line,
            pl.BlockSpec((blocks, per_block, tile), lambda i: (0, 0, jnp.minimum(i, steps - 1))),
            wspec, wspec, wspec,
        ],
        out_specs=[
            pl.BlockSpec((pieces, stacked, slots), lambda i: (0, 0, 0)),
        ]
        + [
            pl.BlockSpec(
                (pieces // SIDE, 2, slots // pieces, tile),
                lambda i: (0, 0, 0, jnp.maximum(i - steps, 0)),
            )
        ]
        * SIDE,
        out_shape=[
            jax.ShapeDtypeStruct((pieces, stacked, slots), BF16),
        ]
        + [jax.ShapeDtypeStruct((pieces // SIDE, 2, slots // pieces, features), BF16)] * SIDE,
        scratch_shapes=[
            pltpu.VMEM((2 * hidden, tokens), F32),
            pltpu.VMEM((hidden, tokens), F32),
            pltpu.VMEM((slots, hidden), BF16),
            pltpu.VMEM((3, slots, hidden), BF16),
            pltpu.VMEM((steps, 3, hidden, tile), BF16),
        ],
        compiler_params=PARAMS,
        cost_estimate=pl.CostEstimate(
            flops=6 * tokens * features * hidden,
            bytes_accessed=33 * 1024 * 1024,
            transcendentals=tokens * hidden,
        ),
        name="expert",
    )(position, place, prob, rows, wg, wu, wd)


def pick_kernel(place_ref, rows_ref, x_ref, g_ref):
    x, g = split_rows(rows_ref)
    pick = one_hot_rows(place_ref[...], x_ref.shape[0])
    x_ref[...] = jnp.dot(pick, x, preferred_element_type=F32).astype(BF16)
    g_ref[...] = jnp.dot(pick, g, preferred_element_type=F32).astype(BF16)


def pick_rows(place, rows):
    blocks, per_block, features = rows.shape
    slots = blocks * CAP
    tokens = place.shape[1]
    steps = 4
    tile = features // steps
    spec = pl.BlockSpec((slots, tile), lambda i: (0, i))
    return pl.pallas_call(
        pick_kernel,
        grid=(steps,),
        in_specs=[
            pl.BlockSpec((1, tokens), lambda i: (0, 0)),
            pl.BlockSpec((blocks, per_block, tile), lambda i: (0, 0, i)),
        ],
        out_specs=[spec, spec],
        out_shape=[jax.ShapeDtypeStruct((slots, features), BF16)] * 2,
        compiler_params=PARAMS,
        cost_estimate=pl.CostEstimate(
            flops=4 * slots * tokens * features, bytes_accessed=24 * 1024 * 1024, transcendentals=0
        ),
        name="pick_rows",
    )(place, rows)


def first_sum_kernel(position_ref, *refs):
    half = len(refs) // 2
    total, outs = refs[-1], refs[half:-1]
    total[...] = sum(ref[...].astype(F32) for ref in refs[:half])
    for distance, ref in enumerate(outs):
        ref[...] = total[lax.rem(position_ref[0] + distance, len(outs))].astype(BF16)


def first_sum(position, got):
    parts, _, height, features = got[0].shape
    steps = 4
    tile = features // steps
    return pl.pallas_call(
        first_sum_kernel,
        grid=(steps,),
        in_specs=[
            pl.BlockSpec(memory_space=pltpu.SMEM),
        ]
        + [pl.BlockSpec((parts, 2, height, tile), lambda i: (0, 0, 0, i))] * parts,
        out_specs=[pl.BlockSpec((2, height, tile), lambda i: (0, 0, i))] * parts,
        out_shape=[jax.ShapeDtypeStruct((2, height, features), BF16)] * parts,
        scratch_shapes=[pltpu.VMEM((parts, 2, height, tile), F32)],
        compiler_params=SMALL,
        name="first_sum",
    )(position, *got)


def gather_kernel(*refs):
    ret_ref = refs[-1]
    total = sum(ref[...].astype(F32) for ref in refs[:-1])
    experts, padded, tile = ret_ref.shape
    blank = jnp.zeros((padded // 2 - CAP, tile), F32)
    for block in range(experts):
        rows = []
        for o in range(2):
            rows += [total[o, block * CAP : (block + 1) * CAP], blank]
        ret_ref[block] = jnp.concatenate(rows, axis=0).astype(BF16)


def gather_blocks(got, experts):
    _, height, features = got[0].shape
    steps = 4
    tile = features // steps
    return pl.pallas_call(
        gather_kernel,
        grid=(steps,),
        in_specs=[pl.BlockSpec((2, height, tile), lambda i: (0, 0, i))] * len(got),
        out_specs=pl.BlockSpec((experts, 8, tile), lambda i: (0, 0, i)),
        out_shape=jax.ShapeDtypeStruct((experts, 8, features), BF16),
        compiler_params=SMALL,
        name="gather_blocks",
    )(*got)


def combine_kernel(chosen_ref, got_ref, mixed_ref, grad_ref):
    experts = got_ref.shape[0]
    for o, ref in enumerate((mixed_ref, grad_ref)):
        total = jnp.zeros(ref.shape, F32)
        for e in range(experts):
            rows = got_ref[e].astype(F32)
            chosen = chosen_ref[e]
            for s in range(CAP):
                total = total + chosen[:, s : s + 1] * rows[4 * o + s : 4 * o + s + 1]
        ref[...] = total.astype(BF16)


def combine(chosen, got):
    experts, padded, features = got.shape
    tokens = chosen.shape[1]
    steps = 2
    tile = features // steps
    spec = pl.BlockSpec((tokens, tile), lambda i: (0, i))
    return pl.pallas_call(
        combine_kernel,
        grid=(steps,),
        in_specs=[
            pl.BlockSpec((experts, tokens, CAP), lambda i: (0, 0, 0)),
            pl.BlockSpec((experts, padded, tile), lambda i: (0, 0, i)),
        ],
        out_specs=[spec, spec],
        out_shape=[jax.ShapeDtypeStruct((tokens, features), BF16)] * 2,
        compiler_params=SMALL,
        name="combine",
    )(chosen, got)


def weights_kernel(lhs_ref, x_ref, g_ref, gate_ref, up_ref, down_ref):
    pieces, stacked, slots = lhs_ref.shape
    rows = stacked // 3
    lhs = lhs_ref[...].astype(F32)
    for n, (src, dst) in enumerate(((x_ref, gate_ref), (x_ref, up_ref), (g_ref, down_ref))):
        part = lhs[:, n * rows : (n + 1) * rows].reshape(pieces * rows, slots).astype(BF16)
        dst[...] = jnp.dot(part, src[...], preferred_element_type=F32).astype(BF16)


def weight_grads(lhs, x, g):
    pieces, stacked, slots = lhs.shape
    features = x.shape[1]
    rows = stacked // 3
    tile = features // 8
    ispec = pl.BlockSpec((slots, tile), lambda i: (0, i))
    ospec = pl.BlockSpec((pieces * rows, tile), lambda i: (0, i))
    oshape = jax.ShapeDtypeStruct((pieces * rows, features), BF16)
    return pl.pallas_call(
        weights_kernel,
        grid=(features // tile,),
        in_specs=[pl.BlockSpec((pieces, stacked, slots), lambda i: (0, 0, 0)), ispec, ispec],
        out_specs=[ospec] * 3,
        out_shape=[oshape] * 3,
        compiler_params=PARAMS,
        cost_estimate=pl.CostEstimate(
            flops=6 * slots * features * pieces * rows,
            bytes_accessed=16 * 1024 * 1024,
            transcendentals=0,
        ),
        name="weight_grads",
    )(lhs, x, g)


def route_places(ids, probs, expert, wide):
    named = ids == expert
    mine = jnp.any(named, axis=2)
    weight = jnp.sum(jnp.where(named, probs, 0.0), axis=2)
    blocks, tokens = mine.shape
    earlier = jnp.arange(tokens)[:, None] < jnp.arange(tokens)[None, :]
    slot = jnp.sum(mine[:, :, None] & earlier[None], axis=1)
    block = jnp.arange(blocks)
    column, branch = block % wide, block // wide
    turned = column % SIDE * SIDE + column // SIDE
    group = jnp.where(expert % 2 == 0, column, turned)
    start = (group * (blocks // wide) + branch) * CAP
    place = jnp.where(mine, start[:, None] + slot, -1)
    return place.astype(jnp.int32).reshape(1, blocks * tokens), weight


def stage_groups(experts, wide, odd):
    groups = []
    for branch in range(experts):
        for k in range(SIDE):
            fast = branch % 2 != odd
            members = [k * SIDE + n if fast else n * SIDE + k for n in range(SIDE)]
            groups.append([branch * wide + m for m in members])
    return groups


def exchange(value, axis):
    return lax.all_to_all(value, axis, split_axis=0, concat_axis=0, tiled=True)


def on_device(x_tokens, out_grad, expert_ids, gate_probs, w_gate, w_up, w_down, attn_out):
    experts = lax.axis_size("branch")
    wide = lax.axis_size("wide")
    blocks = experts * wide
    tokens, features = x_tokens.shape
    both = ("branch", "wide")
    branch_index = lax.axis_index("branch")
    wide_index = lax.axis_index("wide")

    gathered = lax.all_gather(
        jnp.concatenate([x_tokens, out_grad], axis=0), both, axis=0, tiled=True
    )
    gathered = gathered.reshape(blocks, 2 * tokens, features)

    meta = jnp.concatenate([expert_ids.astype(F32), gate_probs], axis=1)
    meta = jnp.pad(meta, ((0, 0), (0, 124)))
    meta = exchange(jnp.broadcast_to(meta[None], (blocks,) + meta.shape), both)
    ids = meta[:, :, 0:2].astype(jnp.int32)
    probs = meta[:, :, 2:4]
    place, weight = route_places(ids, probs, branch_index, wide)
    other_place, _ = route_places(ids, probs, wide_index // (wide // experts), wide)

    scaled = (attn_out[0].astype(F32) * (1.0 / experts)).astype(BF16)
    gathered, scaled = lax.optimization_barrier((gathered, scaled))

    slow, fast = wide_index // SIDE, wide_index % SIDE
    even = branch_index % 2 == 0
    position_one = jnp.where(even, slow, fast).astype(jnp.int32).reshape(1)
    position_two = jnp.where(even, fast, slow).astype(jnp.int32).reshape(1)

    send, *chunks = expert(
        position_one,
        place,
        weight.reshape(1, -1),
        gathered,
        w_gate[0],
        w_up[0],
        w_down[0],
        wide,
    )

    def deliver(parts, odd):
        groups = stage_groups(experts, wide, odd)
        got = [parts[0]]
        for distance in range(1, SIDE):
            pairs = [(g[n], g[(n + distance) % SIDE]) for g in groups for n in range(SIDE)]
            got.append(lax.ppermute(parts[distance], both, pairs))
        return got

    first = deliver(chunks, 0)
    mine = exchange(send, "branch")
    xe, ge = pick_rows(other_place, gathered)
    first, mine, scaled, xe, ge = lax.optimization_barrier((first, mine, scaled, xe, ge))
    merged_attn = lax.psum_scatter(scaled, "branch", scatter_dimension=0, tiled=True)
    sums, mine = lax.optimization_barrier((first_sum(position_two, first), mine))
    relayed = exchange(mine, "wide")
    second = deliver(sums, 1)
    returned = gather_blocks(second, experts)
    grad_gate, grad_up, grad_down = weight_grads(relayed, xe, ge)
    got = exchange(returned, "branch")

    named = jnp.any(expert_ids[None] == jnp.arange(experts)[:, None, None], axis=2)
    earlier = jnp.arange(tokens)[:, None] < jnp.arange(tokens)[None, :]
    slot = jnp.sum(named[:, :, None] & earlier[None], axis=1)
    chosen = named[:, :, None] & (slot[:, :, None] == jnp.arange(CAP)[None, None, :])
    mixed, token_grad = combine(chosen.astype(F32), got)

    layout = (1, 1, wide, w_gate.shape[1] // wide, features)
    return (
        mixed,
        token_grad,
        merged_attn,
        grad_gate.reshape(layout),
        grad_up.reshape(layout),
        grad_down.reshape(layout),
    )


def solution(mesh):
    in_specs = (
        P(("branch", "wide"), None),
        P(("branch", "wide"), None),
        P(("branch", "wide"), None),
        P(("branch", "wide"), None),
        P("branch", "wide", None),
        P("branch", "wide", None),
        P("branch", "wide", None),
        P("branch", None, "wide"),
    )
    out_specs = (
        P(("branch", "wide"), None),
        P(("branch", "wide"), None),
        P("branch", "wide"),
        P("wide", "branch", None, None, None),
        P("wide", "branch", None, None, None),
        P("wide", "branch", None, None, None),
    )
    return jax.shard_map(
        on_device, mesh=mesh, in_specs=in_specs, out_specs=out_specs, check_vma=False
    )
```
